512 devices in a mesh: lat: 4 (over x_hi, core), lon: 128 (over z, y, x_lo).
Axes of the slice: x: 4 (x_hi: 2, x_lo: 2; x = x_hi * 2 + x_lo), y: 8, z: 8, core: 2. Of those that a mesh axis runs over, the one named last changes fastest.
Arguments:
- atmosphere: float32 [256, 1024, 256], P('lat', 'lon'), may hold values from -6 to 6
- disc_basis: float32 [3, 256, 5, 5], P(None, 'lat'), may hold values from -1.25 to 1.25
- polar_basis: float32 [2, 3, 2, 4, 1024], replicated, may hold values from -0.09375 to 0.09375
- widths: int32 [256], P('lat'), may hold values from 0 to 2
- weights: float32 [1, 3, 256, 256], P(None, None, 'lat'), may hold values from -0.21875 to 0.21875
- channel_bias: float32 [1, 256], replicated, may hold values from -3 to 3
Outputs:
- forecast: float32 [256, 1024, 256], P('lat', 'lon')
The draws below stay inside these ranges and needn't reach their ends.
All inputs are finite; a program needn't handle non-finite values.
Results may differ from the reference program's by a relative error of at most 0.0001.
Values sent between devices are 32-bit elements; how exact they have to be, the bound alone decides.
A program may use at most 128 MiB of HBM per device.

```python
import jax
import jax.numpy as jnp
from jax import lax

C = 256
K = 3
REACH = 2
P_SIZE = 2
LAYERS = 1
SOURCE_ROWS = 4
NLAT = 256
NLON = 1024


def draw_widths(key, part):
    key = jax.random.fold_in(key, 7)
    drawn = jax.random.randint(key, (NLAT,), 0, REACH + 1)
    row_ids = jnp.arange(NLAT)
    drawn = jnp.where(row_ids == NLAT // 2, REACH, drawn)
    drawn = jnp.where(row_ids == NLAT // 2 + 1, 0, drawn)
    return drawn.astype(jnp.int32)


def shard_levels(own_key, shape, cuts, smallest, high):
    def one(axis_at, blocks):
        steps = jax.random.uniform(jax.random.fold_in(jax.random.fold_in(own_key, 6), axis_at), (blocks,), jnp.float32, smallest / len(cuts), high / len(cuts))
        return jnp.repeat(jnp.exp(steps), shape[axis_at] // blocks).reshape((-1,) + (1,) * (len(shape) - axis_at - 1))

    factor_of = one(*cuts[0])
    for cut in cuts[1:]:
        factor_of = factor_of * one(*cut)
    return factor_of


def centred(rng, dims, width, limit, pieces=(), held_as=jnp.bfloat16):
    factor_of = shard_levels(rng, dims, pieces, -0.22, 0.18) if pieces else 1.0
    result = jax.random.normal(rng, dims, jnp.float32) * width * factor_of
    return jnp.minimum(jnp.maximum(result, -limit), limit).astype(held_as)


def setup_inputs(seed: int = 0) -> dict:
    seeds = jax.random.split(jax.random.key(seed), 7)
    atmosphere = centred(seeds[0], (NLAT, NLON, C), 1.0, 6.0, ((0, 4), (1, 128)), jnp.float32)
    disc_basis = centred(seeds[1], (K, NLAT, 2 * REACH + 1, 2 * REACH + 1), ((2 * REACH + 1) * (2 * REACH + 1)) ** -0.5, 1.25, ((1, 4),), jnp.float32)
    polar_basis = centred(seeds[2], (2, K, P_SIZE, SOURCE_ROWS, NLON), (SOURCE_ROWS * NLON) ** -0.5, 0.09375, (), jnp.float32)
    widths = draw_widths(jax.random.fold_in(seeds[6], 71), 0)
    weights = centred(seeds[4], (LAYERS, K, C, C), (K * C) ** -0.5, 0.21875, ((2, 4),), jnp.float32)
    channel_bias = centred(seeds[5], (LAYERS, C), 0.5, 3.0, (), jnp.float32)
    return dict(atmosphere=atmosphere, disc_basis=disc_basis, polar_basis=polar_basis, widths=widths, weights=weights, channel_bias=channel_bias)


def polar_term(sources, basis_half, gaps, mixing):
    kernel = basis_half[:, :, :, gaps]
    partial_taps = jnp.einsum("kpqjn,qnc->kpjc", kernel, sources, precision=lax.Precision.HIGHEST)
    return jnp.einsum("kpjc,kcd->pjd", partial_taps, mixing, precision=lax.Precision.HIGHEST)


def reference(atmosphere, disc_basis, polar_basis, widths, weights, channel_bias):
    lat_total, lon_total, channels = atmosphere.shape
    reach_rows = (disc_basis.shape[2] - 1) // 2
    polar_count = polar_basis.shape[2]
    source_count = polar_basis.shape[3]
    offsets = jnp.abs(jnp.arange(2 * reach_rows + 1) - reach_rows)
    taps_mask = (offsets[None, :] <= widths[:, None]).astype(jnp.float32)
    columns = jnp.arange(lon_total, dtype=jnp.int32)
    gaps = ((columns[None, :] - columns[:, None]) % lon_total).astype(jnp.int32)
    state = atmosphere
    for layer_index in range(weights.shape[0]):
        mixing = weights[layer_index]
        padded = jnp.pad(state, ((reach_rows, reach_rows), (0, 0), (0, 0)))
        mixed = jnp.zeros((lat_total * lon_total, channels), jnp.float32)
        for basis_index in range(disc_basis.shape[0]):
            summed = jnp.zeros_like(state)
            for row_step in range(2 * reach_rows + 1):
                rows_block = padded[row_step:row_step + lat_total]
                for col_step in range(2 * reach_rows + 1):
                    weight_row = disc_basis[basis_index, :, row_step, col_step] * taps_mask[:, col_step]
                    summed = summed + weight_row[:, None, None] * jnp.roll(rows_block, reach_rows - col_step, axis=1)
            mixed = mixed + jnp.dot(summed.reshape(-1, channels), mixing[basis_index], precision=lax.Precision.HIGHEST)
        mixed = mixed.reshape(lat_total, lon_total, channels)
        north_part = polar_term(state[:source_count], polar_basis[0], gaps, mixing)
        south_part = polar_term(state[lat_total - source_count:][::-1], polar_basis[1], gaps, mixing)
        mixed = jnp.concatenate([north_part, mixed[polar_count:lat_total - polar_count], south_part[::-1]], axis=0)
        state = jax.nn.gelu(mixed + channel_bias[layer_index], approximate=False)
    return state
```

```python
import jax
import jax.numpy as jnp
from jax import lax
from jax.experimental import pallas as pl
from jax.experimental.pallas import tpu as pltpu
from jax.sharding import PartitionSpec as P

MESH = pl.DeviceIdType.MESH
F32 = jnp.float32
BF16 = jnp.bfloat16

ROWS, COLS, CH = 64, 8, 256
BASES = 3
TILE = 16
TILES = ROWS // TILE
GROUPS = (ROWS + 4) // 4
RING = 8
PLANE = 16
LON = RING * PLANE
LAT = 4


def split(x):
    hi = x.astype(BF16)
    return hi, (x - hi.astype(F32)).astype(BF16)


def dot3(a, b):
    def dot(x, y):
        return jnp.dot(x, y, preferred_element_type=F32)

    return dot(a[0], b[0]) + (dot(a[0], b[1]) + dot(a[1], b[0]))


def gelu(x):
    return 0.5 * x * (1.0 + lax.erf(x * 0.7071067811865476))


def iota(shape, dim):
    return lax.broadcasted_iota(jnp.int32, shape, dim)


def spread(ref, lead, row):
    return jnp.broadcast_to(ref[lead, pl.ds(row, 1), :], (8, 128))


def build_base(disc, wid, flip_main, flip_edge, main, edge):
    flip_main[...] = jnp.zeros_like(flip_main)
    flip_edge[...] = jnp.zeros_like(flip_edge)
    width = wid[...]
    for b in range(5):
        keep = (width >= abs(b - 2)).astype(F32)
        for k in range(BASES):
            for a in range(5):
                row = disc[a, b, k : k + 1, :] * keep
                at = (8 * a + b - 2) % 128
                flip_main[k, at : at + 1, 0:ROWS] = row
                if b < 2:
                    at = 32 + 2 * a + b
                    flip_edge[k, at : at + 1, 0:ROWS] = row
                if b > 2:
                    at = 65 + 2 * a + b - 3
                    flip_edge[k, at : at + 1, 0:ROWS] = row
    for k in range(BASES):
        main[k] = flip_main[k].T[0:ROWS]
        edge[k] = flip_edge[k].T[0:ROWS]


def build_band(main, edge, band):
    sub, lane = iota((8, 128), 0), iota((8, 128), 1)
    near = jnp.abs(lane % 8 - sub) <= 2
    side = ((sub < 2) & (lane < 64)) | ((sub >= 6) & (lane >= 64))
    odd = lane % 2 == 1
    fits = (sub == 0) | (sub == 7) | ((sub == 1) & odd) | ((sub == 6) & ~odd)
    low = lane < 32

    def step(n, carry):
        k, s = n // TILES, n % TILES
        for i in range(TILE):
            row = s * TILE + i
            m = pltpu.roll(spread(main, k, row), 8 * i, 1, stride=1, stride_axis=0)
            m = jnp.where(near, m, 0.0)
            h = jnp.where(side, spread(edge, k, row), 0.0)
            h = jnp.where(fits, pltpu.roll(h, 2 * i, 1, stride=1, stride_axis=0), 0.0)
            if i >= TILE - 4:
                h = jnp.where(low, m, h)
                m = jnp.where(low, 0.0, m)
            at = pl.multiple_of(k * TILE * 8, 8) + 8 * i
            band[s, pl.ds(at, 8), 0:128] = m
            band[s, pl.ds(at, 8), 128:256] = h
        return carry

    lax.fori_loop(0, BASES * TILES, step, 0)


def build_shifts(polar, rows, near, far, z):
    for k in range(BASES):
        for p in range(2):
            at = (2 * k + p) * 4
            rows[at : at + 4, :] = polar[k, p]
    lane = iota((24, 128), 1)
    parts = [rows[:, 128 * d : 128 * d + 128] for d in range(RING)]
    bits = [(lane // (8 * 2**b)) % 2 == 1 for b in range(3)]
    for b in range(3):
        turned = list(parts)
        for d in range(RING):
            if (d >> b) & 1 == 0:
                e = d + 2**b
                shift = 8 * 2**b
                turned[d] = jnp.where(bits[b], pltpu.roll(parts[e], shift, 1), parts[d])
                turned[e] = jnp.where(bits[b], parts[e], pltpu.roll(parts[d], 128 - shift, 1))
        parts = turned
    lower = lane < 64
    for t in range(PLANE):
        v = parts[t % 8]
        other = pltpu.roll(v, 64, 1)
        v = jnp.where(lower, v, other) if t < 8 else jnp.where(lower, other, v)
        here = pltpu.roll(v, 8 * z, 1)
        after = pltpu.roll(here, 8, 1)
        before = pltpu.roll(here, 120, 1)
        near[PLANE + t] = here
        near[t] = after
        far[PLANE + t] = before
        far[t] = here


def build_circular(near, far, circ, g, south):
    sub, lane = iota((8, 128), 0), iota((8, 128), 1)
    over = lane % 8 + sub >= 8
    last = (lane // 8) % 8 == 7
    upper = (lane >= 64) ^ (last & over)

    def step(out_g, carry):
        at = PLANE + g - out_g
        for k in range(BASES):
            for h in range(2):
                blocks = []
                for p in range(2):
                    first = (2 * k + p) * 4
                    q0 = first + 2 * h + south * (3 - 4 * h)
                    q1 = first + 2 * h + 1 + south * (1 - 4 * h)
                    a = jnp.where(upper, spread(near, at, q1), spread(near, at, q0))
                    b = jnp.where(upper, spread(far, at - 1, q1), spread(far, at - 1, q0))
                    v = jnp.where(over, b, a)
                    blocks.append(pltpu.roll(v, 0, 1, stride=1, stride_axis=0))
                circ[k, pl.ds(pl.multiple_of(out_g * 16, 16), 16), 128 * h : 128 * h + 128] = jnp.concatenate(blocks, axis=0)
        return carry

    lax.fori_loop(0, PLANE, step, 0)


def pack(xp, left, right):
    sub = iota((8, CH), 0)

    def place(rows, shifts):
        total = jnp.zeros((8, CH), F32)
        for r in range(4):
            if rows[r] is not None:
                moved = pltpu.roll(rows[r], shifts[r], 0) if shifts[r] else rows[r]
                total = jnp.where(sub // 2 == r, moved, total)
        return total

    def group(t, rows):
        left[t] = place(rows, (0, 2, 4, 6))
        right[t] = place(rows, (2, 4, 6, 0))

    group(0, [None, None, xp[2], xp[3]])
    group(GROUPS - 1, [xp[64], xp[65], None, None])

    def step(t, carry):
        group(t, [xp[4 * t + r] for r in range(4)])
        return carry

    lax.fori_loop(1, GROUPS - 1, step, 0)


def kernel(
    atm, disc_in, polar_in, wid_in, w_in, bias, out,
    xp, lsend, rsend, lrecv, rrecv, corner, disc, polar, wid, wall, whi, wlo,
    flip_main, flip_edge, main, edge, band, xz, prow, near, far, circ, mixp, rs, obuf,
    lsem, osem, halo_s, halo_r, wsem_s, wsem_r, zsem_s, zsem_r, rsem_s, rsem_r,
):
    lat, lon = lax.axis_index("lat"), lax.axis_index("lon")
    z, g = lon // PLANE, lon % PLANE
    before, after = (lon + LON - 1) % LON, (lon + 1) % LON
    sibling = lat + 1 - 2 * (lat % 2)
    across = ((lat + 2) % LAT, lon + 1 - 2 * (lon % 2))
    south = lat // (LAT - 1)
    has_up, has_down = lat > 0, lat < LAT - 1
    is_polar = (lat == 0) | (lat == LAT - 1)
    up, down = jnp.maximum(lat - 1, 0), jnp.minimum(lat + 1, LAT - 1)

    def local(src, dst, n):
        return pltpu.make_async_copy(src, dst, lsem.at[n])

    source_row = south * (ROWS - 4)
    load_x = local(atm, xp.at[pl.ds(2, ROWS)], 0)
    load_w = local(w_in.at[0], wall.at[:, pl.ds(pl.multiple_of(64 * lat, 64), 64)], 1)
    load_d = local(disc_in, disc, 2)
    load_wid = local(wid_in, wid, 3)
    load_p = local(polar_in.at[south], polar, 4)
    load_z = local(atm.at[pl.ds(source_row, 4)], xz.at[:, z], 5)
    for c in (load_x, load_d, load_wid, load_w):
        c.start()

    def remote(src, dst, s, r, device):
        return pltpu.make_async_remote_copy(src, dst, s, r, device_id=device, device_id_type=MESH)

    def ring(d):
        return (lat, ((z + d) % RING) * PLANE + g)

    def plane(d):
        return (lat, z * PLANE + (g + d) % PLANE)

    barrier = pltpu.get_barrier_semaphore()

    def greet(device):
        pl.semaphore_signal(barrier, inc=1, device_id=device, device_id_type=MESH)

    @pl.when(is_polar)
    def _():
        load_p.start()
        load_z.start()
        for d in range(1, RING):
            greet(ring(d))
        for d in range(1, PLANE):
            greet(plane(d))

    for device in ((lat, before), (lat, after), (sibling, lon), across):
        greet(device)

    @pl.when(has_up)
    def _():
        for column in (lon, before, after):
            greet((up, column))

    @pl.when(has_down)
    def _():
        for column in (lon, before, after):
            greet((down, column))

    load_x.wait()
    pack(xp, lsend, rsend)

    pl.semaphore_wait(barrier, 4 + 3 * (has_up.astype(jnp.int32) + has_down.astype(jnp.int32)) + 22 * is_polar.astype(jnp.int32))

    def gather(d):
        return remote(atm.at[pl.ds(source_row, 4)], xz.at[:, z], zsem_s.at[d], zsem_r.at[d], ring(d))

    def shard(n, source_lat, device):
        rows = pl.ds(pl.multiple_of(64 * source_lat, 64), 64)
        return remote(wall.at[:, rows], wall.at[:, rows], wsem_s.at[n], wsem_r.at[n], device)

    own_across = shard(0, lat, across)
    own_sibling = shard(1, lat, (sibling, lon))
    passed_on = shard(2, (lat + 2) % LAT, (sibling, lon))
    to_left = remote(lsend, rrecv, halo_s.at[0], halo_r.at[0], (lat, before))
    to_right = remote(rsend, lrecv, halo_s.at[1], halo_r.at[1], (lat, after))
    to_up = [
        remote(atm.at[pl.ds(0, 2)], xp.at[pl.ds(ROWS + 2, 2)], halo_s.at[2], halo_r.at[2], (up, lon)),
        remote(lsend.at[0], corner.at[3], halo_s.at[3], halo_r.at[3], (up, before)),
        remote(rsend.at[0], corner.at[2], halo_s.at[4], halo_r.at[4], (up, after)),
    ]
    to_down = [
        remote(atm.at[pl.ds(ROWS - 2, 2)], xp.at[pl.ds(0, 2)], halo_s.at[5], halo_r.at[5], (down, lon)),
        remote(lsend.at[GROUPS - 1], corner.at[1], halo_s.at[6], halo_r.at[6], (down, before)),
        remote(rsend.at[GROUPS - 1], corner.at[0], halo_s.at[7], halo_r.at[7], (down, after)),
    ]

    @pl.when(is_polar)
    def _():
        for d in (4, 3, 5, 2, 6, 1, 7):
            gather(d).start()

    load_w.wait()
    own_across.start()
    to_left.start()
    to_right.start()
    own_sibling.start()

    @pl.when(has_up)
    def _():
        for c in to_up:
            c.start()

    @pl.when(has_down)
    def _():
        for c in to_down:
            c.start()

    load_d.wait()
    load_wid.wait()
    build_base(disc, wid, flip_main, flip_edge, main, edge)
    build_band(main, edge, band)

    @pl.when(is_polar)
    def _():
        load_p.wait()
        build_shifts(polar, prow, near, far, z)
        build_circular(near, far, circ, g, south)

    own_across.wait_recv()
    passed_on.start()
    own_sibling.wait_recv()
    passed_on.wait_recv()
    for k in range(BASES):
        hi, lo = split(wall[k])
        whi[CH * k : CH * k + CH, :] = hi
        wlo[CH * k : CH * k + CH, :] = lo

    def mix(taps):
        return dot3(split(jnp.concatenate(taps, axis=1)), (whi[...], wlo[...]))

    def partial(d):
        rows = pl.ds(pl.multiple_of(16 * ((g + d) % PLANE), 16), 16)
        return remote(mixp.at[rows], rs.at[d], rsem_s.at[d], rsem_r.at[d], plane(d))

    @pl.when(is_polar)
    def _():
        load_z.wait()
        for d in range(1, RING):
            gather(d).wait_recv()
        sources = split(xz[...].reshape(CH, CH))
        mixp[...] = mix([dot3(split(circ[k]), sources) for k in range(BASES)])
        for d in (8, 7, 9, 6, 10, 5, 11, 4, 12, 3, 13, 2, 14, 1, 15):
            partial(d).start()

    to_left.wait_recv()
    to_right.wait_recv()
    sub = iota((8, CH), 0)

    @pl.when(has_up)
    def _():
        for c in to_down:
            c.wait_recv()
        lrecv[0] = jnp.where(sub < 4, corner[0], lrecv[0])
        rrecv[0] = jnp.where(sub < 4, corner[1], rrecv[0])

    @pl.when(jnp.logical_not(has_up))
    def _():
        xp[0:2] = jnp.zeros((2, COLS, CH), F32)

    @pl.when(has_down)
    def _():
        for c in to_up:
            c.wait_recv()
        lrecv[GROUPS - 1] = jnp.where(sub < 4, lrecv[GROUPS - 1], corner[2])
        rrecv[GROUPS - 1] = jnp.where(sub < 4, rrecv[GROUPS - 1], corner[3])

    @pl.when(jnp.logical_not(has_down))
    def _():
        xp[ROWS + 2 : ROWS + 4] = jnp.zeros((2, COLS, CH), F32)

    shift = bias[...]
    empty = jnp.zeros((16, CH), F32)
    stores = []

    def store(start, count, n):
        return pltpu.make_async_copy(obuf.at[pl.ds(start, count)], out.at[pl.ds(start, count)], osem.at[n])

    for s in range(TILES):
        x = jnp.concatenate(
            [
                xp[TILE * s : TILE * s + TILE + 4].reshape(160, CH),
                lrecv[4 * s : 4 * s + 5].reshape(40, CH),
                rrecv[4 * s : 4 * s + 5].reshape(40, CH),
                empty,
            ],
            axis=0,
        )
        taps = dot3(split(band[s]), split(x))
        mixed = mix([taps[128 * k : 128 * k + 128] for k in range(BASES)])
        obuf[TILE * s : TILE * s + TILE] = gelu(mixed + shift).reshape(TILE, COLS, CH)
        first, end = max(TILE * s, 2), min(TILE * s + TILE, ROWS - 2)
        stores.append(store(first, end - first, s))
        stores[-1].start()

    @pl.when(is_polar)
    def _():
        total = mixp[pl.ds(pl.multiple_of(16 * g, 16), 16), :]
        for d in range(1, PLANE):
            partial(d).wait_recv()
            total = total + rs[d]
        total = gelu(total + shift)
        for p in range(2):
            obuf[p + south * (ROWS - 1 - 2 * p)] = total[8 * p : 8 * p + 8]

    for start, n in ((0, TILES), (ROWS - 2, TILES + 1)):
        stores.append(store(start, 2, n))
        stores[-1].start()

    for c in (own_across, own_sibling, passed_on, to_left, to_right):
        c.wait_send()

    @pl.when(has_up)
    def _():
        for c in to_up:
            c.wait_send()

    @pl.when(has_down)
    def _():
        for c in to_down:
            c.wait_send()

    @pl.when(is_polar)
    def _():
        for d in range(1, RING):
            gather(d).wait_send()
        for d in range(1, PLANE):
            partial(d).wait_send()

    for c in stores:
        c.wait()


def on_device(atmosphere, disc_basis, polar_basis, widths, weights, channel_bias):
    anywhere = pl.BlockSpec(memory_space=pl.ANY)
    block = jax.ShapeDtypeStruct((ROWS, COLS, CH), F32)

    def vmem(*shape, dtype=F32):
        return pltpu.VMEM(shape, dtype)

    dma = pltpu.SemaphoreType.DMA
    return pl.pallas_call(
        kernel,
        out_shape=block,
        in_specs=[anywhere] * 5 + [pl.BlockSpec(memory_space=pltpu.VMEM)],
        out_specs=anywhere,
        scratch_shapes=[
            vmem(ROWS + 4, COLS, CH),
            vmem(GROUPS, 8, CH),
            vmem(GROUPS, 8, CH),
            vmem(GROUPS, 8, CH),
            vmem(GROUPS, 8, CH),
            vmem(4, 8, CH),
            vmem(5, 5, BASES, ROWS),
            vmem(BASES, 2, 4, 1024),
            vmem(1, ROWS, dtype=jnp.int32),
            vmem(BASES, CH, CH),
            vmem(BASES * CH, CH, dtype=BF16),
            vmem(BASES * CH, CH, dtype=BF16),
            vmem(BASES, 128, 128),
            vmem(BASES, 128, 128),
            vmem(BASES, ROWS, 128),
            vmem(BASES, ROWS, 128),
            vmem(TILES, BASES * TILE * 8, 256),
            vmem(4, RING, 8, CH),
            vmem(24, 1024),
            vmem(2 * PLANE, 24, 128),
            vmem(2 * PLANE, 24, 128),
            vmem(BASES, 256, 256),
            vmem(256, CH),
            vmem(PLANE, 16, CH),
            vmem(ROWS, COLS, CH),
            dma((6,)),
            dma((TILES + 2,)),
            dma((8,)),
            dma((8,)),
            dma((3,)),
            dma((3,)),
            dma((RING,)),
            dma((RING,)),
            dma((PLANE,)),
            dma((PLANE,)),
        ],
        compiler_params=pltpu.CompilerParams(
            collective_id=0, has_side_effects=True, vmem_limit_bytes=40 * 1024 * 1024
        ),
        name="disco",
    )(
        atmosphere,
        jnp.transpose(disc_basis, (2, 3, 0, 1)),
        polar_basis,
        widths.reshape(1, ROWS),
        weights,
        channel_bias,
    )


def solution(mesh):
    return jax.shard_map(
        on_device,
        mesh=mesh,
        in_specs=(
            P("lat", "lon", None),
            P(None, "lat", None, None),
            P(),
            P("lat"),
            P(None, None, "lat", None),
            P(),
        ),
        out_specs=P("lat", "lon", None),
        check_vma=False,
    )
```

```python
import jax
import jax.numpy as jnp
from jax import lax
from jax.experimental import pallas as pl
from jax.experimental.pallas import tpu as pltpu
from jax.sharding import PartitionSpec as P

MESH = pl.DeviceIdType.MESH
F32 = jnp.float32
BF16 = jnp.bfloat16

ROWS, COLS, CH = 64, 8, 256
BASES = 3
TILE = 16
TILES = ROWS // TILE
GROUPS = (ROWS + 4) // 4
RING = 8
PLANE = 16
LON = RING * PLANE
LAT = 4


def split(x):
    hi = x.astype(BF16)
    return hi, (x - hi.astype(F32)).astype(BF16)


def dot3(a, b):
    def dot(x, y):
        return jnp.dot(x, y, preferred_element_type=F32)

    return dot(a[0], b[0]) + (dot(a[0], b[1]) + dot(a[1], b[0]))


def gelu(x):
    return 0.5 * x * (1.0 + lax.erf(x * 0.7071067811865476))


def iota(shape, dim):
    return lax.broadcasted_iota(jnp.int32, shape, dim)


def spread(ref, lead, row):
    return jnp.broadcast_to(ref[lead, pl.ds(row, 1), :], (8, 128))


def build_base(disc, wid, flip_main, flip_edge, main, edge):
    flip_main[...] = jnp.zeros_like(flip_main)
    flip_edge[...] = jnp.zeros_like(flip_edge)
    width = wid[...]
    for b in range(5):
        keep = (width >= abs(b - 2)).astype(F32)
        for k in range(BASES):
            for a in range(5):
                row = disc[a, b, k : k + 1, :] * keep
                at = (8 * a + b - 2) % 128
                flip_main[k, at : at + 1, 0:ROWS] = row
                if b < 2:
                    at = 32 + 2 * a + b
                    flip_edge[k, at : at + 1, 0:ROWS] = row
                if b > 2:
                    at = 65 + 2 * a + b - 3
                    flip_edge[k, at : at + 1, 0:ROWS] = row
    for k in range(BASES):
        main[k] = flip_main[k].T[0:ROWS]
        edge[k] = flip_edge[k].T[0:ROWS]


def build_band(main, edge, band):
    sub, lane = iota((8, 128), 0), iota((8, 128), 1)
    near = jnp.abs(lane % 8 - sub) <= 2
    side = ((sub < 2) & (lane < 64)) | ((sub >= 6) & (lane >= 64))
    odd = lane % 2 == 1
    fits = (sub == 0) | (sub == 7) | ((sub == 1) & odd) | ((sub == 6) & ~odd)
    low = lane < 32

    def step(n, carry):
        k, s = n // TILES, n % TILES
        for i in range(TILE):
            row = s * TILE + i
            m = pltpu.roll(spread(main, k, row), 8 * i, 1, stride=1, stride_axis=0)
            m = jnp.where(near, m, 0.0)
            h = jnp.where(side, spread(edge, k, row), 0.0)
            h = jnp.where(fits, pltpu.roll(h, 2 * i, 1, stride=1, stride_axis=0), 0.0)
            if i >= TILE - 4:
                h = jnp.where(low, m, h)
                m = jnp.where(low, 0.0, m)
            at = pl.multiple_of(k * TILE * 8, 8) + 8 * i
            band[s, pl.ds(at, 8), 0:128] = m
            band[s, pl.ds(at, 8), 128:256] = h
        return carry

    lax.fori_loop(0, BASES * TILES, step, 0)


def build_shifts(polar, rows, near, far, z):
    for k in range(BASES):
        for p in range(2):
            at = (2 * k + p) * 4
            rows[at : at + 4, :] = polar[k, p]
    lane = iota((24, 128), 1)
    parts = [rows[:, 128 * d : 128 * d + 128] for d in range(RING)]
    bits = [(lane // (8 * 2**b)) % 2 == 1 for b in range(3)]
    for b in range(3):
        turned = list(parts)
        for d in range(RING):
            if (d >> b) & 1 == 0:
                e = d + 2**b
                shift = 8 * 2**b
                turned[d] = jnp.where(bits[b], pltpu.roll(parts[e], shift, 1), parts[d])
                turned[e] = jnp.where(bits[b], parts[e], pltpu.roll(parts[d], 128 - shift, 1))
        parts = turned
    lower = lane < 64
    for t in range(PLANE):
        v = parts[t % 8]
        other = pltpu.roll(v, 64, 1)
        v = jnp.where(lower, v, other) if t < 8 else jnp.where(lower, other, v)
        here = pltpu.roll(v, 8 * z, 1)
        after = pltpu.roll(here, 8, 1)
        before = pltpu.roll(here, 120, 1)
        near[PLANE + t] = here
        near[t] = after
        far[PLANE + t] = before
        far[t] = here


def distance(n):
    return PLANE // 2 + (n + 1) // 2 * (1 - 2 * (n % 2))


def build_circular(near, far, chi, clo, g, south):
    sub, lane = iota((8, 128), 0), iota((8, 128), 1)
    over = lane % 8 + sub >= 8
    last = (lane // 8) % 8 == 7
    upper = (lane >= 64) ^ (last & over)

    def step(n, carry):
        at = PLANE + g - (g + distance(n)) % PLANE
        for k in range(BASES):
            for h in range(2):
                blocks = []
                for p in range(2):
                    first = (2 * k + p) * 4
                    q0 = first + 2 * h + south * (3 - 4 * h)
                    q1 = first + 2 * h + 1 + south * (1 - 4 * h)
                    a = jnp.where(upper, spread(near, at, q1), spread(near, at, q0))
                    b = jnp.where(upper, spread(far, at - 1, q1), spread(far, at - 1, q0))
                    v = jnp.where(over, b, a)
                    blocks.append(pltpu.roll(v, 0, 1, stride=1, stride_axis=0))
                rows = pl.ds(pl.multiple_of(n * 16, 16), 16)
                hi, lo = split(jnp.concatenate(blocks, axis=0))
                chi[k, rows, 128 * h : 128 * h + 128] = hi
                clo[k, rows, 128 * h : 128 * h + 128] = lo
        return carry

    lax.fori_loop(0, PLANE, step, 0)


def pack(xp, left, right):
    sub = iota((8, CH), 0)

    def place(rows, shifts):
        total = jnp.zeros((8, CH), F32)
        for r in range(4):
            if rows[r] is not None:
                moved = pltpu.roll(rows[r], shifts[r], 0) if shifts[r] else rows[r]
                total = jnp.where(sub // 2 == r, moved, total)
        return total

    def group(t, rows):
        left[t] = place(rows, (0, 2, 4, 6))
        right[t] = place(rows, (2, 4, 6, 0))

    group(0, [None, None, xp[2], xp[3]])
    group(GROUPS - 1, [xp[64], xp[65], None, None])

    def step(t, carry):
        group(t, [xp[4 * t + r] for r in range(4)])
        return carry

    lax.fori_loop(1, GROUPS - 1, step, 0)


def kernel(
    atm, disc_in, polar_in, wid_in, w_in, bias_in, out,
    xp, lsend, rsend, lrecv, rrecv, corner, disc, polar, wid, bias, wall, whi, wlo,
    flip_main, flip_edge, main, edge, band, xz, prow, near, far, chi, clo, mixp, rs,
    lsem, halo_s, halo_r, wsem_s, wsem_r, zsem_s, zsem_r, rsem_s, rsem_r,
):
    lat, lon = lax.axis_index("lat"), lax.axis_index("lon")
    z, g = lon // PLANE, lon % PLANE
    before, after = (lon + LON - 1) % LON, (lon + 1) % LON
    sibling = lat + 1 - 2 * (lat % 2)
    across = ((lat + 2) % LAT, lon + 1 - 2 * (lon % 2))
    south = lat // (LAT - 1)
    has_up, has_down = lat > 0, lat < LAT - 1
    first, last = lon == 0, lon == LON - 1
    is_polar = (lat == 0) | (lat == LAT - 1)
    up, down = jnp.maximum(lat - 1, 0), jnp.minimum(lat + 1, LAT - 1)

    def local(src, dst, n):
        return pltpu.make_async_copy(src, dst, lsem.at[n])

    source_row = south * (ROWS - 4)
    load_x = local(atm, xp.at[pl.ds(2, ROWS)], 0)
    load_w = local(w_in.at[0], wall.at[:, pl.ds(pl.multiple_of(64 * lat, 64), 64)], 1)
    load_d = local(disc_in, disc, 2)
    load_wid = local(wid_in, wid, 3)
    load_p = local(polar_in.at[south], polar, 4)
    load_b = local(bias_in, bias, 6)
    load_z = local(atm.at[pl.ds(source_row, 4)], xz.at[:, z], 5)

    def remote(src, dst, s, r, device):
        return pltpu.make_async_remote_copy(src, dst, s, r, device_id=device, device_id_type=MESH)

    def ring(d):
        return (lat, ((z + d) % RING) * PLANE + g)

    def plane(d):
        return (lat, z * PLANE + (g + d) % PLANE)

    barrier = pltpu.get_barrier_semaphore()

    def greet(device):
        pl.semaphore_signal(barrier, inc=1, device_id=device, device_id_type=MESH)

    early = z < RING // 2

    def early_at(d):
        return (z + d) % RING < RING // 2

    @pl.when(is_polar)
    def _():
        for n in range(PLANE - 1):
            greet(plane(distance(n)))

    for device in ((sibling, lon), across, (lat, before)):
        greet(device)

    @pl.when(jnp.logical_not(last))
    def _():
        greet((lat, after))

    for there, row in ((has_up, up), (has_down, down)):

        @pl.when(there)
        def _(row=row):
            greet((row, lon))
            greet((row, before))

        @pl.when(there & jnp.logical_not(last))
        def _(row=row):
            greet((row, after))

    @pl.when(is_polar)
    def _():
        for d in range(1, RING):

            @pl.when(early | jnp.logical_not(early_at(d)))
            def _(d=d):
                greet(ring(d))

        load_p.start()
        load_z.start()

    for c in (load_x, load_d, load_wid, load_w, load_b):
        c.start()

    def prepare():
        load_d.wait()
        load_wid.wait()
        build_base(disc, wid, flip_main, flip_edge, main, edge)
        build_band(main, edge, band)

        @pl.when(is_polar)
        def _():
            load_p.wait()
            build_shifts(polar, prow, near, far, z)
            build_circular(near, far, chi, clo, g, south)

    @pl.when(early)
    def _():
        load_x.wait()
        pack(xp, lsend, rsend)
        prepare()

    def count(condition):
        return condition.astype(jnp.int32)

    pl.semaphore_wait(
        barrier,
        4 - count(first) + (3 - count(first)) * (count(has_up) + count(has_down)) + (PLANE + 6 - 4 * count(early)) * count(is_polar),
    )

    def gather(d):
        return remote(atm.at[pl.ds(source_row, 4)], xz.at[:, z], zsem_s.at[d], zsem_r.at[d], ring(d))

    def shard(k, n, source_lat, device):
        rows = pl.ds(pl.multiple_of(64 * source_lat, 64), 64)
        source = wall.at[k, rows] if n == 2 else w_in.at[0, k]
        return remote(source, wall.at[k, rows], wsem_s.at[k, n], wsem_r.at[k, n], device)

    own_across = [shard(k, 0, lat, across) for k in range(BASES)]
    own_sibling = [shard(k, 1, lat, (sibling, lon)) for k in range(BASES)]
    passed_on = [shard(k, 2, (lat + 2) % LAT, (sibling, lon)) for k in range(BASES)]
    to_left = remote(lsend, rrecv, halo_s.at[0], halo_r.at[0], (lat, before))
    to_right = remote(rsend, lrecv, halo_s.at[1], halo_r.at[1], (lat, after))
    to_up = [
        remote(atm.at[pl.ds(0, 2)], xp.at[pl.ds(ROWS + 2, 2)], halo_s.at[2], halo_r.at[2], (up, lon)),
        remote(lsend.at[0], corner.at[3], halo_s.at[3], halo_r.at[3], (up, before)),
        remote(rsend.at[0], corner.at[2], halo_s.at[4], halo_r.at[4], (up, after)),
    ]
    to_down = [
        remote(atm.at[pl.ds(ROWS - 2, 2)], xp.at[pl.ds(0, 2)], halo_s.at[5], halo_r.at[5], (down, lon)),
        remote(lsend.at[GROUPS - 1], corner.at[1], halo_s.at[6], halo_r.at[6], (down, before)),
        remote(rsend.at[GROUPS - 1], corner.at[0], halo_s.at[7], halo_r.at[7], (down, after)),
    ]

    @pl.when(is_polar)
    def _():
        for d in (4, 3, 5, 2, 6, 1, 7):

            @pl.when(early_at(d) | jnp.logical_not(early))
            def _(d=d):
                gather(d).start()

    for c in own_across:
        c.start()

    @pl.when(jnp.logical_not(early))
    def _():
        load_x.wait()
        pack(xp, lsend, rsend)

    to_right.start()

    @pl.when(jnp.logical_not(first))
    def _():
        to_left.start()

    for c in own_sibling:
        c.start()

    for there, copies in ((has_up, to_up), (has_down, to_down)):

        @pl.when(there)
        def _(copies=copies):
            copies[0].start()
            copies[2].start()

        @pl.when(there & jnp.logical_not(first))
        def _(copies=copies):
            copies[1].start()

    @pl.when(jnp.logical_not(early))
    def _():
        prepare()

    for c, d in zip(own_across, passed_on):
        c.wait_recv()
        d.start()

    load_w.wait()
    for k in range(BASES):
        own_sibling[k].wait_recv()
        passed_on[k].wait_recv()
        hi, lo = split(wall[k])
        whi[CH * k : CH * k + CH, :] = hi
        wlo[CH * k : CH * k + CH, :] = lo

    def mix(taps):
        return dot3(split(taps), (whi[...], wlo[...]))

    def partial(n):
        d = distance(n)
        return remote(mixp.at[pl.ds(16 * n, 16)], rs.at[n], rsem_s.at[n], rsem_r.at[n], plane(d))

    @pl.when(is_polar)
    def _():
        load_z.wait()
        for d in (4, 5, 3, 6, 2, 7, 1):
            gather(d).wait_recv()

            @pl.when(early & jnp.logical_not(early_at(RING - d)))
            def _(d=d):
                gather(RING - d).start()

        sources = split(xz[...].reshape(CH, CH))
        for half in range(2):
            rows = slice(128 * half, 128 * half + 128)
            taps = [dot3((chi[k, rows], clo[k, rows]), sources) for k in range(BASES)]
            mixp[rows] = mix(jnp.concatenate(taps, axis=1))
            for n in range(8 * half, min(8 * half + 8, PLANE - 1)):
                partial(n).start()

    to_right.wait_recv()

    @pl.when(first)
    def _():
        to_left.start()

    to_left.wait_recv()
    sub = iota((8, CH), 0)

    @pl.when(has_up)
    def _():
        for c in to_down:
            c.wait_recv()

        @pl.when(first)
        def _():
            to_up[1].start()

        lrecv[0] = jnp.where(sub < 4, corner[0], lrecv[0])
        rrecv[0] = jnp.where(sub < 4, corner[1], rrecv[0])

    @pl.when(jnp.logical_not(has_up))
    def _():
        xp[0:2] = jnp.zeros((2, COLS, CH), F32)

    @pl.when(has_down)
    def _():
        for c in to_up:
            c.wait_recv()

        @pl.when(first)
        def _():
            to_down[1].start()

        lrecv[GROUPS - 1] = jnp.where(sub < 4, lrecv[GROUPS - 1], corner[2])
        rrecv[GROUPS - 1] = jnp.where(sub < 4, rrecv[GROUPS - 1], corner[3])

    @pl.when(jnp.logical_not(has_down))
    def _():
        xp[ROWS + 2 : ROWS + 4] = jnp.zeros((2, COLS, CH), F32)

    load_b.wait()
    shift = bias[...]
    empty = jnp.zeros((16, CH), F32)
    for s in range(TILES):
        x = jnp.concatenate(
            [
                xp[TILE * s : TILE * s + TILE + 4].reshape(160, CH),
                lrecv[4 * s : 4 * s + 5].reshape(40, CH),
                rrecv[4 * s : 4 * s + 5].reshape(40, CH),
                empty,
            ],
            axis=0,
        )
        tile = dot3(split(band[s]), split(x))
        mixed = mix(jnp.concatenate([tile[128 * k : 128 * k + 128] for k in range(BASES)], axis=1))
        out[TILE * s : TILE * s + TILE] = gelu(mixed + shift).reshape(TILE, COLS, CH)

    @pl.when(is_polar)
    def _():
        total = mixp[16 * PLANE - 16 : 16 * PLANE, :]
        for n in range(PLANE - 1):
            partial(n).wait_recv()
            total = total + rs[n]
        total = gelu(total + shift)
        for p in range(2):
            out[p + south * (ROWS - 1 - 2 * p)] = total[8 * p : 8 * p + 8]

    for c in own_across + own_sibling + passed_on + [to_left, to_right]:
        c.wait_send()

    @pl.when(has_up)
    def _():
        for c in to_up:
            c.wait_send()

    @pl.when(has_down)
    def _():
        for c in to_down:
            c.wait_send()

    @pl.when(is_polar)
    def _():
        for d in range(1, RING):
            gather(d).wait_send()
        for n in range(PLANE - 1):
            partial(n).wait_send()


def on_device(atmosphere, disc_basis, polar_basis, widths, weights, channel_bias):
    anywhere = pl.BlockSpec(memory_space=pltpu.MemorySpace.HBM)

    def in_hbm(x):
        return pltpu.with_memory_space_constraint(x, pltpu.MemorySpace.HBM)


    def vmem(*shape, dtype=F32):
        return pltpu.VMEM(shape, dtype)

    dma = pltpu.SemaphoreType.DMA
    return pl.pallas_call(
        kernel,
        out_shape=pltpu.VMEM((ROWS, COLS, CH), F32),
        in_specs=[anywhere] * 6,
        out_specs=pl.BlockSpec(memory_space=pltpu.VMEM),
        scratch_shapes=[
            vmem(ROWS + 4, COLS, CH),
            vmem(GROUPS, 8, CH),
            vmem(GROUPS, 8, CH),
            vmem(GROUPS, 8, CH),
            vmem(GROUPS, 8, CH),
            vmem(4, 8, CH),
            vmem(5, 5, BASES, ROWS),
            vmem(BASES, 2, 4, 1024),
            vmem(1, ROWS, dtype=jnp.int32),
            vmem(1, CH),
            vmem(BASES, CH, CH),
            vmem(BASES * CH, CH, dtype=BF16),
            vmem(BASES * CH, CH, dtype=BF16),
            vmem(BASES, 128, 128),
            vmem(BASES, 128, 128),
            vmem(BASES, ROWS, 128),
            vmem(BASES, ROWS, 128),
            vmem(TILES, BASES * TILE * 8, 256),
            vmem(4, RING, 8, CH),
            vmem(24, 1024),
            vmem(2 * PLANE, 24, 128),
            vmem(2 * PLANE, 24, 128),
            vmem(BASES, 256, 256, dtype=BF16),
            vmem(BASES, 256, 256, dtype=BF16),
            vmem(256, CH),
            vmem(PLANE, 16, CH),
            dma((7,)),
            dma((8,)),
            dma((8,)),
            dma((BASES, 3)),
            dma((BASES, 3)),
            dma((RING,)),
            dma((RING,)),
            dma((PLANE,)),
            dma((PLANE,)),
        ],
        compiler_params=pltpu.CompilerParams(
            collective_id=0, has_side_effects=True, vmem_limit_bytes=32 * 1024 * 1024
        ),
        name="disco",
    )(
        in_hbm(atmosphere),
        in_hbm(jnp.transpose(disc_basis, (2, 3, 0, 1))),
        in_hbm(polar_basis),
        in_hbm(widths.reshape(1, ROWS)),
        in_hbm(weights),
        in_hbm(channel_bias),
    )


def solution(mesh):
    return jax.shard_map(
        on_device,
        mesh=mesh,
        in_specs=(
            P("lat", "lon", None),
            P(None, "lat", None, None),
            P(),
            P("lat"),
            P(None, None, "lat", None),
            P(),
        ),
        out_specs=P("lat", "lon", None),
        check_vma=False,
    )
```

```python
import jax
import jax.numpy as jnp
from jax import lax
from jax.experimental import pallas as pl
from jax.experimental.pallas import tpu as pltpu
from jax.sharding import PartitionSpec as P

MESH = pl.DeviceIdType.MESH
F32 = jnp.float32
BF16 = jnp.bfloat16

ROWS, COLS, CH = 64, 8, 256
BASES = 3
TILE = 16
TILES = ROWS // TILE
GROUPS = (ROWS + 4) // 4
RING = 8
PLANE = 16
LON = RING * PLANE
LAT = 4


def split(x):
    hi = x.astype(BF16)
    return hi, (x - hi.astype(F32)).astype(BF16)


def dot3(a, b):
    def dot(x, y):
        return jnp.dot(x, y, preferred_element_type=F32)

    return dot(a[0], b[0]) + (dot(a[0], b[1]) + dot(a[1], b[0]))


def gelu(x):
    return 0.5 * x * (1.0 + lax.erf(x * 0.7071067811865476))


def iota(shape, dim):
    return lax.broadcasted_iota(jnp.int32, shape, dim)


def spread(ref, lead, row):
    return jnp.broadcast_to(ref[lead, pl.ds(row, 1), :], (8, 128))


def build_base(disc, wid, flip_main, flip_edge, main, edge):
    flip_main[...] = jnp.zeros_like(flip_main)
    flip_edge[...] = jnp.zeros_like(flip_edge)
    width = wid[...]
    for b in range(5):
        keep = (width >= abs(b - 2)).astype(F32)
        for k in range(BASES):
            for a in range(5):
                row = disc[a, b, k : k + 1, :] * keep
                at = (8 * a + b - 2) % 128
                flip_main[k, at : at + 1, 0:ROWS] = row
                if b < 2:
                    at = 32 + 2 * a + b
                    flip_edge[k, at : at + 1, 0:ROWS] = row
                if b > 2:
                    at = 65 + 2 * a + b - 3
                    flip_edge[k, at : at + 1, 0:ROWS] = row
    for k in range(BASES):
        main[k] = flip_main[k].T[0:ROWS]
        edge[k] = flip_edge[k].T[0:ROWS]


def build_band(main, edge, band):
    sub, lane = iota((8, 128), 0), iota((8, 128), 1)
    near = jnp.abs(lane % 8 - sub) <= 2
    side = ((sub < 2) & (lane < 64)) | ((sub >= 6) & (lane >= 64))
    odd = lane % 2 == 1
    fits = (sub == 0) | (sub == 7) | ((sub == 1) & odd) | ((sub == 6) & ~odd)
    low = lane < 32

    def step(n, carry):
        k, s = n // TILES, n % TILES
        for i in range(TILE):
            row = s * TILE + i
            m = pltpu.roll(spread(main, k, row), 8 * i, 1, stride=1, stride_axis=0)
            m = jnp.where(near, m, 0.0)
            h = jnp.where(side, spread(edge, k, row), 0.0)
            h = jnp.where(fits, pltpu.roll(h, 2 * i, 1, stride=1, stride_axis=0), 0.0)
            if i >= TILE - 4:
                h = jnp.where(low, m, h)
                m = jnp.where(low, 0.0, m)
            at = pl.multiple_of(k * TILE * 8, 8) + 8 * i
            band[s, pl.ds(at, 8), 0:128] = m
            band[s, pl.ds(at, 8), 128:256] = h
        return carry

    lax.fori_loop(0, BASES * TILES, step, 0)


def build_shifts(polar, rows, near, far, z):
    for k in range(BASES):
        for p in range(2):
            at = (2 * k + p) * 4
            rows[at : at + 4, :] = polar[k, p]
    lane = iota((24, 128), 1)
    parts = [rows[:, 128 * d : 128 * d + 128] for d in range(RING)]
    bits = [(lane // (8 * 2**b)) % 2 == 1 for b in range(3)]
    for b in range(3):
        turned = list(parts)
        for d in range(RING):
            if (d >> b) & 1 == 0:
                e = d + 2**b
                shift = 8 * 2**b
                turned[d] = jnp.where(bits[b], pltpu.roll(parts[e], shift, 1), parts[d])
                turned[e] = jnp.where(bits[b], parts[e], pltpu.roll(parts[d], 128 - shift, 1))
        parts = turned
    lower = lane < 64
    for t in range(PLANE):
        v = parts[t % 8]
        other = pltpu.roll(v, 64, 1)
        v = jnp.where(lower, v, other) if t < 8 else jnp.where(lower, other, v)
        here = pltpu.roll(v, 8 * z, 1)
        after = pltpu.roll(here, 8, 1)
        before = pltpu.roll(here, 120, 1)
        near[PLANE + t] = here
        near[t] = after
        far[PLANE + t] = before
        far[t] = here


def distance(n):
    return PLANE // 2 + (n + 1) // 2 * (1 - 2 * (n % 2))


def build_circular(near, far, chi, clo, g, south):
    sub, lane = iota((8, 128), 0), iota((8, 128), 1)
    over = lane % 8 + sub >= 8
    last = (lane // 8) % 8 == 7
    upper = (lane >= 64) ^ (last & over)

    def step(n, carry):
        at = PLANE + g - (g + distance(n)) % PLANE
        for k in range(BASES):
            for h in range(2):
                blocks = []
                for p in range(2):
                    first = (2 * k + p) * 4
                    q0 = first + 2 * h + south * (3 - 4 * h)
                    q1 = first + 2 * h + 1 + south * (1 - 4 * h)
                    a = jnp.where(upper, spread(near, at, q1), spread(near, at, q0))
                    b = jnp.where(upper, spread(far, at - 1, q1), spread(far, at - 1, q0))
                    v = jnp.where(over, b, a)
                    blocks.append(pltpu.roll(v, 0, 1, stride=1, stride_axis=0))
                rows = pl.ds(pl.multiple_of(n * 16, 16), 16)
                hi, lo = split(jnp.concatenate(blocks, axis=0))
                chi[k, rows, 128 * h : 128 * h + 128] = hi
                clo[k, rows, 128 * h : 128 * h + 128] = lo
        return carry

    lax.fori_loop(0, PLANE, step, 0)


def pack(xp, left, right):
    sub = iota((8, CH), 0)

    def place(rows, shifts):
        total = jnp.zeros((8, CH), F32)
        for r in range(4):
            if rows[r] is not None:
                moved = pltpu.roll(rows[r], shifts[r], 0) if shifts[r] else rows[r]
                total = jnp.where(sub // 2 == r, moved, total)
        return total

    def group(t, rows):
        left[t] = place(rows, (0, 2, 4, 6))
        right[t] = place(rows, (2, 4, 6, 0))

    group(0, [None, None, xp[2], xp[3]])
    group(GROUPS - 1, [xp[64], xp[65], None, None])

    def step(t, carry):
        group(t, [xp[4 * t + r] for r in range(4)])
        return carry

    lax.fori_loop(1, GROUPS - 1, step, 0)


def kernel(
    atm, disc_in, polar_in, wid_in, w_in, bias_in, out,
    xp, lsend, rsend, lrecv, rrecv, corner, disc, polar, wid, bias, wall, whi, wlo,
    flip_main, flip_edge, main, edge, band, xz, prow, shift_a, shift_b, chi, clo, mixp, rs,
    lsem, halo_s, halo_r, wsem_s, wsem_r, zsem_s, zsem_r, rsem_s, rsem_r, known, hello, near, seam,
):
    lat, lon = lax.axis_index("lat"), lax.axis_index("lon")
    z, g = lon // PLANE, lon % PLANE
    before, after = (lon + LON - 1) % LON, (lon + 1) % LON
    sibling = lat + 1 - 2 * (lat % 2)
    across = ((lat + 2) % LAT, lon + 1 - 2 * (lon % 2))
    south = lat // (LAT - 1)
    has_up, has_down = lat > 0, lat < LAT - 1
    first, last = lon == 0, lon == LON - 1
    is_polar = (lat == 0) | (lat == LAT - 1)
    up, down = jnp.maximum(lat - 1, 0), jnp.minimum(lat + 1, LAT - 1)

    def local(src, dst, n):
        return pltpu.make_async_copy(src, dst, lsem.at[n])

    source_row = south * (ROWS - 4)
    load_x = local(atm, xp.at[pl.ds(2, ROWS)], 0)
    load_w = local(w_in.at[0], wall.at[:, pl.ds(pl.multiple_of(64 * lat, 64), 64)], 1)
    load_d = local(disc_in, disc, 2)
    load_wid = local(wid_in, wid, 3)
    load_p = local(polar_in.at[south], polar, 4)
    load_b = local(bias_in, bias, 6)
    load_z = local(atm.at[pl.ds(source_row, 4)], xz.at[:, z], 5)

    def remote(src, dst, s, r, device):
        return pltpu.make_async_remote_copy(src, dst, s, r, device_id=device, device_id_type=MESH)

    def ring(d):
        return (lat, ((z + d) % RING) * PLANE + g)

    def plane(d):
        return (lat, z * PLANE + (g + d) % PLANE)

    barrier = pltpu.get_barrier_semaphore()

    def greet(device):
        pl.semaphore_signal(barrier, inc=1, device_id=device, device_id_type=MESH)

    late = z >= RING // 2
    turn = PLANE - 1 - 2 * g
    turning = is_polar & ((g == 0) | (g == PLANE - 1))
    odd = lon % 2 == 1
    whole = lon >= 0

    neighbours = [
        (jnp.logical_not(last), whole, (lat, after)),
        (jnp.logical_not(first), jnp.logical_not(whole), (lat, before)),
        (has_up, jnp.logical_not(whole), (up, lon)),
        (has_down, whole, (down, lon)),
        (has_up & jnp.logical_not(last), whole, (up, after)),
        (has_down & jnp.logical_not(last), whole, (down, after)),
        (has_up & jnp.logical_not(first), jnp.logical_not(whole), (up, before)),
        (has_down & jnp.logical_not(first), jnp.logical_not(whole), (down, before)),
        (whole, jnp.logical_not(odd), across),
        (turning, g == 0, (lat, lon + turn)),
    ]

    def count(*conditions):
        return sum(c.astype(jnp.int32) for c in conditions)

    @pl.when(is_polar)
    def _():
        load_z.start()

    for there, later, device in neighbours:

        @pl.when(there & later)
        def _(device=device):
            greet(device)

    for there, row in ((first, lat), (first & has_up, up), (first & has_down, down)):

        @pl.when(there)
        def _(row=row):
            greet((row, before))

    @pl.when(is_polar)
    def _():
        for d in range(1, RING):

            @pl.when(z + d < RING)
            def _(d=d):
                greet(ring(d))

        load_p.start()

    for c in (load_x, load_d, load_wid, load_w, load_b):
        c.start()

    def prepare_base():
        load_d.wait()
        load_wid.wait()
        build_base(disc, wid, flip_main, flip_edge, main, edge)

    def prepare_band():
        build_band(main, edge, band)

    def prepare_polar():
        load_p.wait()
        build_shifts(polar, prow, shift_a, shift_b, z)
        build_circular(shift_a, shift_b, chi, clo, g, south)

    greeted = count(*[there & jnp.logical_not(later) for there, later, _ in neighbours])
    greeted += count(last, last & has_up, last & has_down) + z * count(is_polar)

    @pl.when(greeted > 0)
    def _():
        pl.semaphore_wait(barrier, greeted)

    def gather(d):
        return remote(xz.at[:, z], xz.at[:, z], zsem_s.at[d], zsem_r.at[d], ring(d))

    def shard(k, n, source_lat, device):
        rows = pl.ds(pl.multiple_of(64 * source_lat, 64), 64)
        source = wall.at[k, rows] if n == 2 else w_in.at[0, k]
        return remote(source, wall.at[k, rows], wsem_s.at[k, n], wsem_r.at[k, n], device)

    own_across = [shard(k, 0, lat, across) for k in range(BASES)]
    own_sibling = [shard(k, 1, lat, (sibling, lon)) for k in range(BASES)]
    passed_on = [shard(k, 2, (lat + 2) % LAT, (sibling, lon)) for k in range(BASES)]
    to_left = remote(lsend, rrecv, halo_s.at[0], halo_r.at[0], (lat, before))
    to_right = remote(rsend, lrecv, halo_s.at[1], halo_r.at[1], (lat, after))
    to_up = [
        remote(atm.at[pl.ds(0, 2)], xp.at[pl.ds(ROWS + 2, 2)], halo_s.at[2], halo_r.at[2], (up, lon)),
        remote(lsend.at[0], corner.at[3], halo_s.at[3], halo_r.at[3], (up, before)),
        remote(rsend.at[0], corner.at[2], halo_s.at[4], halo_r.at[4], (up, after)),
    ]
    to_down = [
        remote(atm.at[pl.ds(ROWS - 2, 2)], xp.at[pl.ds(0, 2)], halo_s.at[5], halo_r.at[5], (down, lon)),
        remote(lsend.at[GROUPS - 1], corner.at[1], halo_s.at[6], halo_r.at[6], (down, before)),
        remote(rsend.at[GROUPS - 1], corner.at[0], halo_s.at[7], halo_r.at[7], (down, after)),
    ]

    @pl.when(is_polar)
    def _():
        for d in range(1, RING):

            @pl.when(z + d >= RING)
            def _(d=d):
                pl.semaphore_signal(hello.at[d], inc=1, device_id=ring(d), device_id_type=MESH)

        load_z.wait()
        for d in (4, 3, 5, 2, 6, 1, 7):

            @pl.when(z + d >= RING)
            def _(d=d):
                gather(d).start()

    for there, later, device in neighbours:

        @pl.when(there & jnp.logical_not(later))
        def _(device=device):
            pl.semaphore_signal(near, inc=1, device_id=device, device_id_type=MESH)

    @pl.when(last)
    def _():
        pl.semaphore_signal(seam.at[0], inc=1, device_id=(lat, after), device_id_type=MESH)

    @pl.when(last & has_up)
    def _():
        pl.semaphore_signal(seam.at[2], inc=1, device_id=(up, after), device_id_type=MESH)

    @pl.when(last & has_down)
    def _():
        pl.semaphore_signal(seam.at[1], inc=1, device_id=(down, after), device_id_type=MESH)

    load_x.wait()
    pack(xp, lsend, rsend)
    to_come = count(*[there & later for there, later, _ in neighbours])

    @pl.when(to_come > 0)
    def _():
        pl.semaphore_wait(near, to_come)

    for c in own_across:
        c.start()

    held_right = late & (g == PLANE - 1) & jnp.logical_not(last)
    held_left = (late & (g == 0)) | last

    @pl.when(jnp.logical_not(held_right))
    def _():
        to_right.start()

    @pl.when(jnp.logical_not(first | held_left))
    def _():
        to_left.start()

    for c in own_sibling:
        c.start()

    for there, copies in ((has_up, to_up), (has_down, to_down)):

        @pl.when(there)
        def _(copies=copies):
            copies[0].start()
            copies[2].start()

        @pl.when(there & jnp.logical_not(first))
        def _(copies=copies):
            copies[1].start()

    def step_out(n):
        for side in range(2):
            there = plane(2**n if side == 0 else PLANE - 2**n)
            pl.semaphore_signal(known.at[n, side], inc=1, device_id=there, device_id_type=MESH)

    def step_in(n):
        for side in range(2):
            pl.semaphore_wait(known.at[n, side], 1)

    def answer():
        for d in range(RING - 1, 0, -1):

            @pl.when(z < d)
            def _(d=d):
                pl.semaphore_wait(hello.at[d], 1)
                gather(RING - d).start()

    @pl.when(is_polar)
    def _():
        step_out(0)

    prepare_base()

    @pl.when(is_polar)
    def _():
        step_in(0)
        step_out(1)

    prepare_band()

    @pl.when(is_polar)
    def _():
        step_in(1)
        step_out(2)

    @pl.when(is_polar)
    def _():
        answer()
        prepare_polar()

    for c, d in zip(own_across, passed_on):
        c.wait_recv()
        d.start()

    for n, there, copy in ((0, first, to_left), (1, first & has_up, to_up[1]), (2, first & has_down, to_down[1])):

        @pl.when(there)
        def _(n=n, copy=copy):
            pl.semaphore_wait(seam.at[n], 1)
            copy.start()

    pl.when(held_right)(to_right.start)
    pl.when(held_left)(to_left.start)
    load_w.wait()
    for k in range(BASES):
        own_sibling[k].wait_recv()
        passed_on[k].wait_recv()
        hi, lo = split(wall[k])
        whi[CH * k : CH * k + CH, :] = hi
        wlo[CH * k : CH * k + CH, :] = lo

    def mix(taps):
        return dot3(split(taps), (whi[...], wlo[...]))

    def partial(n):
        d = distance(n)
        return remote(mixp.at[pl.ds(16 * n, 16)], rs.at[n], rsem_s.at[n], rsem_r.at[n], plane(d))

    @pl.when(is_polar)
    def _():
        for d in range(1, RING):
            gather(d).wait_recv()
        sources = split(xz[...].reshape(CH, CH))
        step_in(2)
        for half in range(2):
            rows = slice(128 * half, 128 * half + 128)
            taps = [dot3((chi[k, rows], clo[k, rows]), sources) for k in range(BASES)]
            mixp[rows] = mix(jnp.concatenate(taps, axis=1))
            for n in range(8 * half, min(8 * half + 8, PLANE - 1)):
                partial(n).start()

    to_right.wait_recv()
    to_left.wait_recv()
    sub = iota((8, CH), 0)

    @pl.when(has_up)
    def _():
        for c in to_down:
            c.wait_recv()
        lrecv[0] = jnp.where(sub < 4, corner[0], lrecv[0])
        rrecv[0] = jnp.where(sub < 4, corner[1], rrecv[0])

    @pl.when(jnp.logical_not(has_up))
    def _():
        xp[0:2] = jnp.zeros((2, COLS, CH), F32)

    @pl.when(has_down)
    def _():
        for c in to_up:
            c.wait_recv()
        lrecv[GROUPS - 1] = jnp.where(sub < 4, lrecv[GROUPS - 1], corner[2])
        rrecv[GROUPS - 1] = jnp.where(sub < 4, rrecv[GROUPS - 1], corner[3])

    @pl.when(jnp.logical_not(has_down))
    def _():
        xp[ROWS + 2 : ROWS + 4] = jnp.zeros((2, COLS, CH), F32)

    load_b.wait()
    shift = bias[...]
    empty = jnp.zeros((16, CH), F32)
    for s in range(TILES):
        x = jnp.concatenate(
            [
                xp[TILE * s : TILE * s + TILE + 4].reshape(160, CH),
                lrecv[4 * s : 4 * s + 5].reshape(40, CH),
                rrecv[4 * s : 4 * s + 5].reshape(40, CH),
                empty,
            ],
            axis=0,
        )
        tile = dot3(split(band[s]), split(x))
        mixed = mix(jnp.concatenate([tile[128 * k : 128 * k + 128] for k in range(BASES)], axis=1))
        out[TILE * s : TILE * s + TILE] = gelu(mixed + shift).reshape(TILE, COLS, CH)

    @pl.when(is_polar)
    def _():
        total = mixp[16 * PLANE - 16 : 16 * PLANE, :]
        for n in range(PLANE - 1):
            partial(n).wait_recv()
            total = total + rs[n]
        total = gelu(total + shift)
        for p in range(2):
            out[p + south * (ROWS - 1 - 2 * p)] = total[8 * p : 8 * p + 8]

    for c in own_across + own_sibling + passed_on + [to_left, to_right]:
        c.wait_send()

    @pl.when(has_up)
    def _():
        for c in to_up:
            c.wait_send()

    @pl.when(has_down)
    def _():
        for c in to_down:
            c.wait_send()

    @pl.when(is_polar)
    def _():
        for d in range(1, RING):
            gather(d).wait_send()
        for n in range(PLANE - 1):
            partial(n).wait_send()


def on_device(atmosphere, disc_basis, polar_basis, widths, weights, channel_bias):
    anywhere = pl.BlockSpec(memory_space=pltpu.MemorySpace.HBM)

    def in_hbm(x):
        return pltpu.with_memory_space_constraint(x, pltpu.MemorySpace.HBM)


    def vmem(*shape, dtype=F32):
        return pltpu.VMEM(shape, dtype)

    dma = pltpu.SemaphoreType.DMA
    return pl.pallas_call(
        kernel,
        out_shape=pltpu.VMEM((ROWS, COLS, CH), F32),
        in_specs=[anywhere] * 6,
        out_specs=pl.BlockSpec(memory_space=pltpu.VMEM),
        scratch_shapes=[
            vmem(ROWS + 4, COLS, CH),
            vmem(GROUPS, 8, CH),
            vmem(GROUPS, 8, CH),
            vmem(GROUPS, 8, CH),
            vmem(GROUPS, 8, CH),
            vmem(4, 8, CH),
            vmem(5, 5, BASES, ROWS),
            vmem(BASES, 2, 4, 1024),
            vmem(1, ROWS, dtype=jnp.int32),
            vmem(1, CH),
            vmem(BASES, CH, CH),
            vmem(BASES * CH, CH, dtype=BF16),
            vmem(BASES * CH, CH, dtype=BF16),
            vmem(BASES, 128, 128),
            vmem(BASES, 128, 128),
            vmem(BASES, ROWS, 128),
            vmem(BASES, ROWS, 128),
            vmem(TILES, BASES * TILE * 8, 256),
            vmem(4, RING, 8, CH),
            vmem(24, 1024),
            vmem(2 * PLANE, 24, 128),
            vmem(2 * PLANE, 24, 128),
            vmem(BASES, 256, 256, dtype=BF16),
            vmem(BASES, 256, 256, dtype=BF16),
            vmem(256, CH),
            vmem(PLANE, 16, CH),
            dma((7,)),
            dma((8,)),
            dma((8,)),
            dma((BASES, 3)),
            dma((BASES, 3)),
            dma((RING,)),
            dma((RING,)),
            dma((PLANE,)),
            dma((PLANE,)),
            pltpu.SemaphoreType.REGULAR((3, 2)),
            pltpu.SemaphoreType.REGULAR((RING,)),
            pltpu.SemaphoreType.REGULAR,
            pltpu.SemaphoreType.REGULAR((3,)),
        ],
        compiler_params=pltpu.CompilerParams(
            collective_id=0, has_side_effects=True, vmem_limit_bytes=32 * 1024 * 1024
        ),
        name="disco",
    )(
        in_hbm(atmosphere),
        in_hbm(jnp.transpose(disc_basis, (2, 3, 0, 1))),
        in_hbm(polar_basis),
        in_hbm(widths.reshape(1, ROWS)),
        in_hbm(weights),
        in_hbm(channel_bias),
    )


def solution(mesh):
    return jax.shard_map(
        on_device,
        mesh=mesh,
        in_specs=(
            P("lat", "lon", None),
            P(None, "lat", None, None),
            P(),
            P("lat"),
            P(None, None, "lat", None),
            P(),
        ),
        out_specs=P("lat", "lon", None),
        check_vma=False,
    )
```

```python
import jax
import jax.numpy as jnp
from jax import lax
from jax.experimental import pallas as pl
from jax.experimental.pallas import tpu as pltpu
from jax.sharding import PartitionSpec as P

MESH = pl.DeviceIdType.MESH
F32 = jnp.float32
BF16 = jnp.bfloat16

ROWS, COLS, CH = 64, 8, 256
BASES = 3
TILE = 16
TILES = ROWS // TILE
GROUPS = (ROWS + 4) // 4
RING = 8
PLANE = 16
LON = RING * PLANE
LAT = 4


def split(x):
    hi = x.astype(BF16)
    return hi, (x - hi.astype(F32)).astype(BF16)


def dot3(a, b):
    def dot(x, y):
        return jnp.dot(x, y, preferred_element_type=F32)

    return dot(a[0], b[0]) + (dot(a[0], b[1]) + dot(a[1], b[0]))


def gelu(x):
    return 0.5 * x * (1.0 + lax.erf(x * 0.7071067811865476))


def iota(shape, dim):
    return lax.broadcasted_iota(jnp.int32, shape, dim)


def spread(ref, lead, row):
    return jnp.broadcast_to(ref[lead, pl.ds(row, 1), :], (8, 128))


def build_base(disc, wid, flip_main, flip_edge, main, edge):
    flip_main[...] = jnp.zeros_like(flip_main)
    flip_edge[...] = jnp.zeros_like(flip_edge)
    width = wid[...]
    for b in range(5):
        keep = (width >= abs(b - 2)).astype(F32)
        for k in range(BASES):
            for a in range(5):
                row = disc[a, b, k : k + 1, :] * keep
                at = (8 * a + b - 2) % 128
                flip_main[k, at : at + 1, 0:ROWS] = row
                if b < 2:
                    at = 32 + 2 * a + b
                    flip_edge[k, at : at + 1, 0:ROWS] = row
                if b > 2:
                    at = 65 + 2 * a + b - 3
                    flip_edge[k, at : at + 1, 0:ROWS] = row
    for k in range(BASES):
        main[k] = flip_main[k].T[0:ROWS]
        edge[k] = flip_edge[k].T[0:ROWS]


def build_band(main, edge, band):
    sub, lane = iota((8, 128), 0), iota((8, 128), 1)
    near = jnp.abs(lane % 8 - sub) <= 2
    side = ((sub < 2) & (lane < 64)) | ((sub >= 6) & (lane >= 64))
    odd = lane % 2 == 1
    fits = (sub == 0) | (sub == 7) | ((sub == 1) & odd) | ((sub == 6) & ~odd)
    low = lane < 32

    def step(n, carry):
        k, s = n // TILES, n % TILES
        for i in range(TILE):
            row = s * TILE + i
            m = pltpu.roll(spread(main, k, row), 8 * i, 1, stride=1, stride_axis=0)
            m = jnp.where(near, m, 0.0)
            h = jnp.where(side, spread(edge, k, row), 0.0)
            h = jnp.where(fits, pltpu.roll(h, 2 * i, 1, stride=1, stride_axis=0), 0.0)
            if i >= TILE - 4:
                h = jnp.where(low, m, h)
                m = jnp.where(low, 0.0, m)
            at = pl.multiple_of(k * TILE * 8, 8) + 8 * i
            band[s, pl.ds(at, 8), 0:128] = m
            band[s, pl.ds(at, 8), 128:256] = h
        return carry

    lax.fori_loop(0, BASES * TILES, step, 0)


def build_shifts(polar, rows, near, far, z):
    for k in range(BASES):
        for p in range(2):
            at = (2 * k + p) * 4
            rows[at : at + 4, :] = polar[k, p]
    lane = iota((24, 128), 1)
    parts = [rows[:, 128 * d : 128 * d + 128] for d in range(RING)]
    bits = [(lane // (8 * 2**b)) % 2 == 1 for b in range(3)]
    for b in range(3):
        turned = list(parts)
        for d in range(RING):
            if (d >> b) & 1 == 0:
                e = d + 2**b
                shift = 8 * 2**b
                turned[d] = jnp.where(bits[b], pltpu.roll(parts[e], shift, 1), parts[d])
                turned[e] = jnp.where(bits[b], parts[e], pltpu.roll(parts[d], 128 - shift, 1))
        parts = turned
    lower = lane < 64
    for t in range(PLANE):
        v = parts[t % 8]
        other = pltpu.roll(v, 64, 1)
        v = jnp.where(lower, v, other) if t < 8 else jnp.where(lower, other, v)
        here = pltpu.roll(v, 8 * z, 1)
        after = pltpu.roll(here, 8, 1)
        before = pltpu.roll(here, 120, 1)
        near[PLANE + t] = here
        near[t] = after
        far[PLANE + t] = before
        far[t] = here


def distance(n):
    return PLANE // 2 + (n + 1) // 2 * (1 - 2 * (n % 2))


def build_circular(near, far, chi, clo, g, south):
    sub, lane = iota((8, 128), 0), iota((8, 128), 1)
    over = lane % 8 + sub >= 8
    last = (lane // 8) % 8 == 7
    upper = (lane >= 64) ^ (last & over)

    def step(n, carry):
        at = PLANE + g - (g + distance(n)) % PLANE
        for k in range(BASES):
            for h in range(2):
                blocks = []
                for p in range(2):
                    first = (2 * k + p) * 4
                    q0 = first + 2 * h + south * (3 - 4 * h)
                    q1 = first + 2 * h + 1 + south * (1 - 4 * h)
                    a = jnp.where(upper, spread(near, at, q1), spread(near, at, q0))
                    b = jnp.where(upper, spread(far, at - 1, q1), spread(far, at - 1, q0))
                    v = jnp.where(over, b, a)
                    blocks.append(pltpu.roll(v, 0, 1, stride=1, stride_axis=0))
                rows = pl.ds(pl.multiple_of(n * 16, 16), 16)
                hi, lo = split(jnp.concatenate(blocks, axis=0))
                chi[k, rows, 128 * h : 128 * h + 128] = hi
                clo[k, rows, 128 * h : 128 * h + 128] = lo
        return carry

    lax.fori_loop(0, PLANE, step, 0)


def pack(xp, left, right):
    sub = iota((8, CH), 0)

    def place(rows, shifts):
        total = jnp.zeros((8, CH), F32)
        for r in range(4):
            if rows[r] is not None:
                moved = pltpu.roll(rows[r], shifts[r], 0) if shifts[r] else rows[r]
                total = jnp.where(sub // 2 == r, moved, total)
        return total

    def group(t, rows):
        left[t] = place(rows, (0, 2, 4, 6))
        right[t] = place(rows, (2, 4, 6, 0))

    group(0, [None, None, xp[2], xp[3]])
    group(GROUPS - 1, [xp[64], xp[65], None, None])

    def step(t, carry):
        group(t, [xp[4 * t + r] for r in range(4)])
        return carry

    lax.fori_loop(1, GROUPS - 1, step, 0)


def kernel(
    atm, disc_in, polar_in, wid_in, w_in, bias_in, out,
    xp, lsend, rsend, lrecv, rrecv, corner, disc, polar, wid, bias, wall, whi, wlo,
    flip_main, flip_edge, main, edge, band, xz, prow, shift_a, shift_b, chi, clo, mixp, rs,
    lsem, halo_s, halo_r, wsem_s, wsem_r, zsem_s, zsem_r, rsem_s, rsem_r, known, hello, near, seam,
):
    lat, lon = lax.axis_index("lat"), lax.axis_index("lon")
    z, g = lon // PLANE, lon % PLANE
    before, after = (lon + LON - 1) % LON, (lon + 1) % LON
    sibling = lat + 1 - 2 * (lat % 2)
    across = ((lat + 2) % LAT, lon + 1 - 2 * (lon % 2))
    south = lat // (LAT - 1)
    has_up, has_down = lat > 0, lat < LAT - 1
    first, last = lon == 0, lon == LON - 1
    is_polar = (lat == 0) | (lat == LAT - 1)
    up, down = jnp.maximum(lat - 1, 0), jnp.minimum(lat + 1, LAT - 1)

    def local(src, dst, n):
        return pltpu.make_async_copy(src, dst, lsem.at[n])

    source_row = south * (ROWS - 4)
    load_x = local(atm, xp.at[pl.ds(2, ROWS)], 0)
    load_w = local(w_in.at[0], wall.at[:, pl.ds(pl.multiple_of(64 * lat, 64), 64)], 1)
    load_d = local(disc_in, disc, 2)
    load_wid = local(wid_in, wid, 3)
    load_p = local(polar_in.at[south], polar, 4)
    load_b = local(bias_in, bias, 6)
    load_z = local(atm.at[pl.ds(source_row, 4)], xz.at[:, z], 5)

    def remote(src, dst, s, r, device):
        return pltpu.make_async_remote_copy(src, dst, s, r, device_id=device, device_id_type=MESH)

    def ring(d):
        return (lat, ((z + d) % RING) * PLANE + g)

    def plane(d):
        return (lat, z * PLANE + (g + d) % PLANE)

    barrier = pltpu.get_barrier_semaphore()

    def greet(device):
        pl.semaphore_signal(barrier, inc=1, device_id=device, device_id_type=MESH)

    late = z >= RING // 2
    turn = PLANE - 1 - 2 * g
    turning = is_polar & ((g == 0) | (g == PLANE - 1))
    odd = lon % 2 == 1
    whole = lon >= 0

    neighbours = [
        (jnp.logical_not(last), whole, (lat, after)),
        (jnp.logical_not(first), jnp.logical_not(whole), (lat, before)),
        (has_up, jnp.logical_not(whole), (up, lon)),
        (has_down, whole, (down, lon)),
        (has_up & jnp.logical_not(last), whole, (up, after)),
        (has_down & jnp.logical_not(last), whole, (down, after)),
        (has_up & jnp.logical_not(first), jnp.logical_not(whole), (up, before)),
        (has_down & jnp.logical_not(first), jnp.logical_not(whole), (down, before)),
        (whole, jnp.logical_not(odd), across),
        (turning, g == 0, (lat, lon + turn)),
    ]

    def count(*conditions):
        return sum(c.astype(jnp.int32) for c in conditions)

    @pl.when(is_polar)
    def _():
        load_z.start()

    for there, later, device in neighbours:

        @pl.when(there & later)
        def _(device=device):
            greet(device)

    for there, row in ((first, lat), (first & has_up, up), (first & has_down, down)):

        @pl.when(there)
        def _(row=row):
            greet((row, before))

    @pl.when(is_polar)
    def _():
        for d in range(1, RING):

            @pl.when(z + d < RING)
            def _(d=d):
                greet(ring(d))

    load_x.start()

    def prepare_base():
        load_d.wait()
        load_wid.wait()
        build_base(disc, wid, flip_main, flip_edge, main, edge)

    def prepare_band():
        build_band(main, edge, band)

    def prepare_polar():
        load_p.wait()
        build_shifts(polar, prow, shift_a, shift_b, z)
        build_circular(shift_a, shift_b, chi, clo, g, south)

    greeted = count(*[there & jnp.logical_not(later) for there, later, _ in neighbours])
    greeted += count(last, last & has_up, last & has_down) + z * count(is_polar)

    @pl.when(greeted > 0)
    def _():
        pl.semaphore_wait(barrier, greeted)

    def gather(d):
        return remote(xz.at[:, z], xz.at[:, z], zsem_s.at[d], zsem_r.at[d], ring(d))

    def shard(k, n, source_lat, device):
        rows = pl.ds(pl.multiple_of(64 * source_lat, 64), 64)
        source = wall.at[k, rows] if n == 2 else w_in.at[0, k]
        return remote(source, wall.at[k, rows], wsem_s.at[k, n], wsem_r.at[k, n], device)

    own_across = [shard(k, 0, lat, across) for k in range(BASES)]
    own_sibling = [shard(k, 1, lat, (sibling, lon)) for k in range(BASES)]
    passed_on = [shard(k, 2, (lat + 2) % LAT, (sibling, lon)) for k in range(BASES)]
    to_left = remote(lsend, rrecv, halo_s.at[0], halo_r.at[0], (lat, before))
    to_right = remote(rsend, lrecv, halo_s.at[1], halo_r.at[1], (lat, after))
    to_up = [
        remote(atm.at[pl.ds(0, 2)], xp.at[pl.ds(ROWS + 2, 2)], halo_s.at[2], halo_r.at[2], (up, lon)),
        remote(lsend.at[0], corner.at[3], halo_s.at[3], halo_r.at[3], (up, before)),
        remote(rsend.at[0], corner.at[2], halo_s.at[4], halo_r.at[4], (up, after)),
    ]
    to_down = [
        remote(atm.at[pl.ds(ROWS - 2, 2)], xp.at[pl.ds(0, 2)], halo_s.at[5], halo_r.at[5], (down, lon)),
        remote(lsend.at[GROUPS - 1], corner.at[1], halo_s.at[6], halo_r.at[6], (down, before)),
        remote(rsend.at[GROUPS - 1], corner.at[0], halo_s.at[7], halo_r.at[7], (down, after)),
    ]

    @pl.when(is_polar)
    def _():
        load_z.wait()
        for d in range(1, RING):

            @pl.when(z + d >= RING)
            def _(d=d):
                gather(d).start()

        for d in range(1, RING):

            @pl.when(z + d >= RING)
            def _(d=d):
                pl.semaphore_signal(hello.at[d], inc=1, device_id=ring(d), device_id_type=MESH)

    for there, later, device in neighbours:

        @pl.when(there & jnp.logical_not(later))
        def _(device=device):
            pl.semaphore_signal(near, inc=1, device_id=device, device_id_type=MESH)

    @pl.when(last)
    def _():
        pl.semaphore_signal(seam.at[0], inc=1, device_id=(lat, after), device_id_type=MESH)

    @pl.when(last & has_up)
    def _():
        pl.semaphore_signal(seam.at[2], inc=1, device_id=(up, after), device_id_type=MESH)

    @pl.when(last & has_down)
    def _():
        pl.semaphore_signal(seam.at[1], inc=1, device_id=(down, after), device_id_type=MESH)

    for c in (load_w, load_d, load_wid, load_b):
        c.start()

    pl.when(is_polar)(load_p.start)
    load_x.wait()
    pack(xp, lsend, rsend)
    to_come = count(*[there & later for there, later, _ in neighbours])

    @pl.when(to_come > 0)
    def _():
        pl.semaphore_wait(near, to_come)

    for c in own_across:
        c.start()

    held_right = late & (g == PLANE - 1) & jnp.logical_not(last)
    held_left = (late & (g == 0)) | last

    @pl.when(jnp.logical_not(held_right))
    def _():
        to_right.start()

    @pl.when(jnp.logical_not(first | held_left))
    def _():
        to_left.start()

    for c in own_sibling:
        c.start()

    for there, copies in ((has_up, to_up), (has_down, to_down)):

        @pl.when(there)
        def _(copies=copies):
            copies[0].start()
            copies[2].start()

        @pl.when(there & jnp.logical_not(first))
        def _(copies=copies):
            copies[1].start()

    def step_out(n):
        for side in range(2):
            there = plane(2**n if side == 0 else PLANE - 2**n)
            pl.semaphore_signal(known.at[n, side], inc=1, device_id=there, device_id_type=MESH)

    def step_in(n):
        for side in range(2):
            pl.semaphore_wait(known.at[n, side], 1)

    def answer():
        for d in range(RING - 1, 0, -1):

            @pl.when(z < d)
            def _(d=d):
                pl.semaphore_wait(hello.at[d], 1)
                gather(RING - d).start()

    @pl.when(is_polar)
    def _():
        step_out(0)

    prepare_base()

    @pl.when(is_polar)
    def _():
        step_in(0)
        step_out(1)

    prepare_band()

    @pl.when(is_polar)
    def _():
        step_in(1)
        step_out(2)

    @pl.when(is_polar)
    def _():
        pl.when(z >= RING // 4)(answer)
        prepare_polar()
        pl.when(z < RING // 4)(answer)

    for c, d in zip(own_across, passed_on):
        c.wait_recv()
        d.start()

    for n, there, copy in ((0, first, to_left), (1, first & has_up, to_up[1]), (2, first & has_down, to_down[1])):

        @pl.when(there)
        def _(n=n, copy=copy):
            pl.semaphore_wait(seam.at[n], 1)
            copy.start()

    pl.when(held_right)(to_right.start)
    pl.when(held_left)(to_left.start)
    load_w.wait()
    for k in range(BASES):
        own_sibling[k].wait_recv()
        passed_on[k].wait_recv()
        hi, lo = split(wall[k])
        whi[CH * k : CH * k + CH, :] = hi
        wlo[CH * k : CH * k + CH, :] = lo

    def mix(taps):
        return dot3(split(taps), (whi[...], wlo[...]))

    def partial(n):
        d = distance(n)
        return remote(mixp.at[pl.ds(16 * n, 16)], rs.at[n], rsem_s.at[n], rsem_r.at[n], plane(d))

    @pl.when(is_polar)
    def _():
        for d in range(1, RING):
            gather(d).wait_recv()
        sources = split(xz[...].reshape(CH, CH))
        step_in(2)
        for half in range(2):
            rows = slice(128 * half, 128 * half + 128)
            taps = [dot3((chi[k, rows], clo[k, rows]), sources) for k in range(BASES)]
            mixp[rows] = mix(jnp.concatenate(taps, axis=1))
            for n in range(8 * half, min(8 * half + 8, PLANE - 1)):
                partial(n).start()

    to_right.wait_recv()
    to_left.wait_recv()
    sub = iota((8, CH), 0)

    @pl.when(has_up)
    def _():
        for c in to_down:
            c.wait_recv()
        lrecv[0] = jnp.where(sub < 4, corner[0], lrecv[0])
        rrecv[0] = jnp.where(sub < 4, corner[1], rrecv[0])

    @pl.when(jnp.logical_not(has_up))
    def _():
        xp[0:2] = jnp.zeros((2, COLS, CH), F32)

    @pl.when(has_down)
    def _():
        for c in to_up:
            c.wait_recv()
        lrecv[GROUPS - 1] = jnp.where(sub < 4, lrecv[GROUPS - 1], corner[2])
        rrecv[GROUPS - 1] = jnp.where(sub < 4, rrecv[GROUPS - 1], corner[3])

    @pl.when(jnp.logical_not(has_down))
    def _():
        xp[ROWS + 2 : ROWS + 4] = jnp.zeros((2, COLS, CH), F32)

    load_b.wait()
    shift = bias[...]
    empty = jnp.zeros((16, CH), F32)
    for s in range(TILES):
        x = jnp.concatenate(
            [
                xp[TILE * s : TILE * s + TILE + 4].reshape(160, CH),
                lrecv[4 * s : 4 * s + 5].reshape(40, CH),
                rrecv[4 * s : 4 * s + 5].reshape(40, CH),
                empty,
            ],
            axis=0,
        )
        tile = dot3(split(band[s]), split(x))
        mixed = mix(jnp.concatenate([tile[128 * k : 128 * k + 128] for k in range(BASES)], axis=1))
        out[TILE * s : TILE * s + TILE] = gelu(mixed + shift).reshape(TILE, COLS, CH)

    @pl.when(is_polar)
    def _():
        total = mixp[16 * PLANE - 16 : 16 * PLANE, :]
        for n in range(PLANE - 1):
            partial(n).wait_recv()
            total = total + rs[n]
        total = gelu(total + shift)
        for p in range(2):
            out[p + south * (ROWS - 1 - 2 * p)] = total[8 * p : 8 * p + 8]

    for c in own_across + own_sibling + passed_on + [to_left, to_right]:
        c.wait_send()

    @pl.when(has_up)
    def _():
        for c in to_up:
            c.wait_send()

    @pl.when(has_down)
    def _():
        for c in to_down:
            c.wait_send()

    @pl.when(is_polar)
    def _():
        for d in range(1, RING):
            gather(d).wait_send()
        for n in range(PLANE - 1):
            partial(n).wait_send()


def on_device(atmosphere, disc_basis, polar_basis, widths, weights, channel_bias):
    anywhere = pl.BlockSpec(memory_space=pltpu.MemorySpace.HBM)

    def in_hbm(x):
        return pltpu.with_memory_space_constraint(x, pltpu.MemorySpace.HBM)


    def vmem(*shape, dtype=F32):
        return pltpu.VMEM(shape, dtype)

    dma = pltpu.SemaphoreType.DMA
    return pl.pallas_call(
        kernel,
        out_shape=pltpu.VMEM((ROWS, COLS, CH), F32),
        in_specs=[anywhere] * 6,
        out_specs=pl.BlockSpec(memory_space=pltpu.VMEM),
        scratch_shapes=[
            vmem(ROWS + 4, COLS, CH),
            vmem(GROUPS, 8, CH),
            vmem(GROUPS, 8, CH),
            vmem(GROUPS, 8, CH),
            vmem(GROUPS, 8, CH),
            vmem(4, 8, CH),
            vmem(5, 5, BASES, ROWS),
            vmem(BASES, 2, 4, 1024),
            vmem(1, ROWS, dtype=jnp.int32),
            vmem(1, CH),
            vmem(BASES, CH, CH),
            vmem(BASES * CH, CH, dtype=BF16),
            vmem(BASES * CH, CH, dtype=BF16),
            vmem(BASES, 128, 128),
            vmem(BASES, 128, 128),
            vmem(BASES, ROWS, 128),
            vmem(BASES, ROWS, 128),
            vmem(TILES, BASES * TILE * 8, 256),
            vmem(4, RING, 8, CH),
            vmem(24, 1024),
            vmem(2 * PLANE, 24, 128),
            vmem(2 * PLANE, 24, 128),
            vmem(BASES, 256, 256, dtype=BF16),
            vmem(BASES, 256, 256, dtype=BF16),
            vmem(256, CH),
            vmem(PLANE, 16, CH),
            dma((7,)),
            dma((8,)),
            dma((8,)),
            dma((BASES, 3)),
            dma((BASES, 3)),
            dma((RING,)),
            dma((RING,)),
            dma((PLANE,)),
            dma((PLANE,)),
            pltpu.SemaphoreType.REGULAR((3, 2)),
            pltpu.SemaphoreType.REGULAR((RING,)),
            pltpu.SemaphoreType.REGULAR,
            pltpu.SemaphoreType.REGULAR((3,)),
        ],
        compiler_params=pltpu.CompilerParams(
            collective_id=0, has_side_effects=True, vmem_limit_bytes=32 * 1024 * 1024
        ),
        name="disco",
    )(
        in_hbm(atmosphere),
        in_hbm(jnp.transpose(disc_basis, (2, 3, 0, 1))),
        in_hbm(polar_basis),
        in_hbm(widths.reshape(1, ROWS)),
        in_hbm(weights),
        in_hbm(channel_bias),
    )


def solution(mesh):
    return jax.shard_map(
        on_device,
        mesh=mesh,
        in_specs=(
            P("lat", "lon", None),
            P(None, "lat", None, None),
            P(),
            P("lat"),
            P(None, None, "lat", None),
            P(),
        ),
        out_specs=P("lat", "lon", None),
        check_vma=False,
    )
```

```python
import jax
import jax.numpy as jnp
from jax import lax
from jax.experimental import pallas as pl
from jax.experimental.pallas import tpu as pltpu
from jax.sharding import PartitionSpec as P

MESH = pl.DeviceIdType.MESH
F32 = jnp.float32
BF16 = jnp.bfloat16

ROWS, COLS, CH = 64, 8, 256
BASES = 3
TILE = 16
TILES = ROWS // TILE
GROUPS = (ROWS + 4) // 4
RING = 8
PLANE = 16
LON = RING * PLANE
LAT = 4


def split(x):
    hi = x.astype(BF16)
    return hi, (x - hi.astype(F32)).astype(BF16)


def dot3(a, b):
    def dot(x, y):
        return jnp.dot(x, y, preferred_element_type=F32)

    return dot(a[0], b[0]) + (dot(a[0], b[1]) + dot(a[1], b[0]))


def gelu(x):
    return 0.5 * x * (1.0 + lax.erf(x * 0.7071067811865476))


def iota(shape, dim):
    return lax.broadcasted_iota(jnp.int32, shape, dim)


def spread(ref, lead, row):
    return jnp.broadcast_to(ref[lead, pl.ds(row, 1), :], (8, 128))


def build_base(disc, wid, flip_main, flip_edge, main, edge):
    flip_main[...] = jnp.zeros_like(flip_main)
    flip_edge[...] = jnp.zeros_like(flip_edge)
    width = wid[...]
    for b in range(5):
        keep = (width >= abs(b - 2)).astype(F32)
        for k in range(BASES):
            for a in range(5):
                row = disc[a, b, k : k + 1, :] * keep
                at = (8 * a + b - 2) % 128
                flip_main[k, at : at + 1, 0:ROWS] = row
                if b < 2:
                    at = 32 + 2 * a + b
                    flip_edge[k, at : at + 1, 0:ROWS] = row
                if b > 2:
                    at = 65 + 2 * a + b - 3
                    flip_edge[k, at : at + 1, 0:ROWS] = row
    for k in range(BASES):
        main[k] = flip_main[k].T[0:ROWS]
        edge[k] = flip_edge[k].T[0:ROWS]


def build_band(main, edge, band):
    sub, lane = iota((8, 128), 0), iota((8, 128), 1)
    near = jnp.abs(lane % 8 - sub) <= 2
    side = ((sub < 2) & (lane < 64)) | ((sub >= 6) & (lane >= 64))
    odd = lane % 2 == 1
    fits = (sub == 0) | (sub == 7) | ((sub == 1) & odd) | ((sub == 6) & ~odd)
    low = lane < 32

    def step(n, carry):
        k, s = n // TILES, n % TILES
        for i in range(TILE):
            row = s * TILE + i
            m = pltpu.roll(spread(main, k, row), 8 * i, 1, stride=1, stride_axis=0)
            m = jnp.where(near, m, 0.0)
            h = jnp.where(side, spread(edge, k, row), 0.0)
            h = jnp.where(fits, pltpu.roll(h, 2 * i, 1, stride=1, stride_axis=0), 0.0)
            if i >= TILE - 4:
                h = jnp.where(low, m, h)
                m = jnp.where(low, 0.0, m)
            at = pl.multiple_of(k * TILE * 8, 8) + 8 * i
            band[s, pl.ds(at, 8), 0:128] = m
            band[s, pl.ds(at, 8), 128:256] = h
        return carry

    lax.fori_loop(0, BASES * TILES, step, 0)


def build_shifts(polar, rows, near, far, z):
    for k in range(BASES):
        for p in range(2):
            at = (2 * k + p) * 4
            rows[at : at + 4, :] = polar[k, p]
    lane = iota((24, 128), 1)
    parts = [rows[:, 128 * d : 128 * d + 128] for d in range(RING)]
    bits = [(lane // (8 * 2**b)) % 2 == 1 for b in range(3)]
    for b in range(3):
        turned = list(parts)
        for d in range(RING):
            if (d >> b) & 1 == 0:
                e = d + 2**b
                shift = 8 * 2**b
                turned[d] = jnp.where(bits[b], pltpu.roll(parts[e], shift, 1), parts[d])
                turned[e] = jnp.where(bits[b], parts[e], pltpu.roll(parts[d], 128 - shift, 1))
        parts = turned
    lower = lane < 64
    for t in range(PLANE):
        v = parts[t % 8]
        other = pltpu.roll(v, 64, 1)
        v = jnp.where(lower, v, other) if t < 8 else jnp.where(lower, other, v)
        here = pltpu.roll(v, 8 * z, 1)
        after = pltpu.roll(here, 8, 1)
        before = pltpu.roll(here, 120, 1)
        near[PLANE + t] = here
        near[t] = after
        far[PLANE + t] = before
        far[t] = here


def distance(n):
    return PLANE // 2 + (n + 1) // 2 * (1 - 2 * (n % 2))


def build_circular(near, far, chi, clo, g, south):
    sub, lane = iota((8, 128), 0), iota((8, 128), 1)
    over = lane % 8 + sub >= 8
    last = (lane // 8) % 8 == 7
    upper = (lane >= 64) ^ (last & over)

    def step(n, carry):
        at = PLANE + g - (g + distance(n)) % PLANE
        for k in range(BASES):
            for h in range(2):
                blocks = []
                for p in range(2):
                    first = (2 * k + p) * 4
                    q0 = first + 2 * h + south * (3 - 4 * h)
                    q1 = first + 2 * h + 1 + south * (1 - 4 * h)
                    a = jnp.where(upper, spread(near, at, q1), spread(near, at, q0))
                    b = jnp.where(upper, spread(far, at - 1, q1), spread(far, at - 1, q0))
                    v = jnp.where(over, b, a)
                    blocks.append(pltpu.roll(v, 0, 1, stride=1, stride_axis=0))
                rows = pl.ds(pl.multiple_of(n * 16, 16), 16)
                hi, lo = split(jnp.concatenate(blocks, axis=0))
                chi[k, rows, 128 * h : 128 * h + 128] = hi
                clo[k, rows, 128 * h : 128 * h + 128] = lo
        return carry

    lax.fori_loop(0, PLANE, step, 0)


def pack(xp, left, right):
    sub = iota((8, CH), 0)

    def place(rows, shifts):
        total = jnp.zeros((8, CH), F32)
        for r in range(4):
            if rows[r] is not None:
                moved = pltpu.roll(rows[r], shifts[r], 0) if shifts[r] else rows[r]
                total = jnp.where(sub // 2 == r, moved, total)
        return total

    def group(t, rows):
        left[t] = place(rows, (0, 2, 4, 6))
        right[t] = place(rows, (2, 4, 6, 0))

    group(0, [None, None, xp[2], xp[3]])
    group(GROUPS - 1, [xp[64], xp[65], None, None])

    def step(t, carry):
        group(t, [xp[4 * t + r] for r in range(4)])
        return carry

    lax.fori_loop(1, GROUPS - 1, step, 0)


def kernel(
    atm, disc_in, polar_in, wid_in, w_in, bias_in, out,
    xp, lsend, rsend, lrecv, rrecv, corner, disc, polar, wid, bias, wall, whi, wlo,
    flip_main, flip_edge, main, edge, band, xz, prow, shift_a, shift_b, chi, clo, mixp, rs,
    lsem, halo_s, halo_r, wsem_s, wsem_r, zsem_s, zsem_r, rsem_s, rsem_r, known, hello, near, seam,
):
    lat, lon = lax.axis_index("lat"), lax.axis_index("lon")
    z, g = lon // PLANE, lon % PLANE
    before, after = (lon + LON - 1) % LON, (lon + 1) % LON
    sibling = lat + 1 - 2 * (lat % 2)
    across = ((lat + 2) % LAT, lon + 1 - 2 * (lon % 2))
    south = lat // (LAT - 1)
    has_up, has_down = lat > 0, lat < LAT - 1
    first, last = lon == 0, lon == LON - 1
    is_polar = (lat == 0) | (lat == LAT - 1)
    up, down = jnp.maximum(lat - 1, 0), jnp.minimum(lat + 1, LAT - 1)

    def local(src, dst, n):
        return pltpu.make_async_copy(src, dst, lsem.at[n])

    source_row = south * (ROWS - 4)
    load_x = local(atm, xp.at[pl.ds(2, ROWS)], 0)
    load_w = local(w_in.at[0], wall.at[:, pl.ds(pl.multiple_of(64 * lat, 64), 64)], 1)
    load_d = local(disc_in, disc, 2)
    load_wid = local(wid_in, wid, 3)
    load_p = local(polar_in.at[south], polar, 4)
    load_b = local(bias_in, bias, 6)
    load_z = local(atm.at[pl.ds(source_row, 4)], xz.at[:, z], 5)

    def remote(src, dst, s, r, device):
        return pltpu.make_async_remote_copy(src, dst, s, r, device_id=device, device_id_type=MESH)

    def ring(d):
        return (lat, ((z + d) % RING) * PLANE + g)

    def plane(d):
        return (lat, z * PLANE + (g + d) % PLANE)

    barrier = pltpu.get_barrier_semaphore()

    def greet(device):
        pl.semaphore_signal(barrier, inc=1, device_id=device, device_id_type=MESH)

    late = z >= RING // 2
    turn = PLANE - 1 - 2 * g
    turning = is_polar & ((g == 0) | (g == PLANE - 1))
    odd = lon % 2 == 1
    whole = lon >= 0

    neighbours = [
        (jnp.logical_not(last), whole, (lat, after)),
        (jnp.logical_not(first), jnp.logical_not(whole), (lat, before)),
        (has_up, jnp.logical_not(whole), (up, lon)),
        (has_down, whole, (down, lon)),
        (has_up & jnp.logical_not(last), whole, (up, after)),
        (has_down & jnp.logical_not(last), whole, (down, after)),
        (has_up & jnp.logical_not(first), jnp.logical_not(whole), (up, before)),
        (has_down & jnp.logical_not(first), jnp.logical_not(whole), (down, before)),
        (whole, jnp.logical_not(odd), across),
        (turning, g == 0, (lat, lon + turn)),
    ]

    def count(*conditions):
        return sum(c.astype(jnp.int32) for c in conditions)

    @pl.when(is_polar)
    def _():
        load_z.start()

    for there, later, device in neighbours:

        @pl.when(there & later)
        def _(device=device):
            greet(device)

    for there, row in ((first, lat), (first & has_up, up), (first & has_down, down)):

        @pl.when(there)
        def _(row=row):
            greet((row, before))

    @pl.when(is_polar)
    def _():
        for d in range(1, RING):

            @pl.when(z + d < RING)
            def _(d=d):
                greet(ring(d))

    load_x.start()

    def prepare_base():
        load_d.wait()
        load_wid.wait()
        build_base(disc, wid, flip_main, flip_edge, main, edge)

    def prepare_band():
        build_band(main, edge, band)

    def prepare_polar():
        load_p.wait()
        build_shifts(polar, prow, shift_a, shift_b, z)
        build_circular(shift_a, shift_b, chi, clo, g, south)

    greeted = count(*[there & jnp.logical_not(later) for there, later, _ in neighbours])
    greeted += count(last, last & has_up, last & has_down) + z * count(is_polar)

    @pl.when(greeted > 0)
    def _():
        pl.semaphore_wait(barrier, greeted)

    def gather(d):
        return remote(xz.at[:, z], xz.at[:, z], zsem_s.at[d], zsem_r.at[d], ring(d))

    def shard(k, n, source_lat, device):
        rows = pl.ds(pl.multiple_of(64 * source_lat, 64), 64)
        source = wall.at[k, rows] if n == 2 else w_in.at[0, k]
        return remote(source, wall.at[k, rows], wsem_s.at[k, n], wsem_r.at[k, n], device)

    own_across = [shard(k, 0, lat, across) for k in range(BASES)]
    own_sibling = [shard(k, 1, lat, (sibling, lon)) for k in range(BASES)]
    passed_on = [shard(k, 2, (lat + 2) % LAT, (sibling, lon)) for k in range(BASES)]
    to_left = remote(lsend, rrecv, halo_s.at[0], halo_r.at[0], (lat, before))
    to_right = remote(rsend, lrecv, halo_s.at[1], halo_r.at[1], (lat, after))
    to_up = [
        remote(atm.at[pl.ds(0, 2)], xp.at[pl.ds(ROWS + 2, 2)], halo_s.at[2], halo_r.at[2], (up, lon)),
        remote(lsend.at[0], corner.at[3], halo_s.at[3], halo_r.at[3], (up, before)),
        remote(rsend.at[0], corner.at[2], halo_s.at[4], halo_r.at[4], (up, after)),
    ]
    to_down = [
        remote(atm.at[pl.ds(ROWS - 2, 2)], xp.at[pl.ds(0, 2)], halo_s.at[5], halo_r.at[5], (down, lon)),
        remote(lsend.at[GROUPS - 1], corner.at[1], halo_s.at[6], halo_r.at[6], (down, before)),
        remote(rsend.at[GROUPS - 1], corner.at[0], halo_s.at[7], halo_r.at[7], (down, after)),
    ]

    @pl.when(is_polar)
    def _():
        load_z.wait()
        for d in range(1, RING):

            @pl.when(z + d >= RING)
            def _(d=d):
                gather(d).start()

        for d in range(1, RING):

            @pl.when(z + d >= RING)
            def _(d=d):
                pl.semaphore_signal(hello.at[d], inc=1, device_id=ring(d), device_id_type=MESH)

    for there, later, device in neighbours:

        @pl.when(there & jnp.logical_not(later))
        def _(device=device):
            pl.semaphore_signal(near, inc=1, device_id=device, device_id_type=MESH)

    @pl.when(last)
    def _():
        pl.semaphore_signal(seam.at[0], inc=1, device_id=(lat, after), device_id_type=MESH)

    @pl.when(last & has_up)
    def _():
        pl.semaphore_signal(seam.at[2], inc=1, device_id=(up, after), device_id_type=MESH)

    @pl.when(last & has_down)
    def _():
        pl.semaphore_signal(seam.at[1], inc=1, device_id=(down, after), device_id_type=MESH)

    for c in (load_w, load_d, load_wid, load_b):
        c.start()

    pl.when(is_polar)(load_p.start)
    load_x.wait()
    pack(xp, lsend, rsend)
    to_come = count(*[there & later for there, later, _ in neighbours])

    @pl.when(to_come > 0)
    def _():
        pl.semaphore_wait(near, to_come)

    for c in own_across:
        c.start()

    held_right = late & (g == PLANE - 1) & jnp.logical_not(last)
    held_left = (late & (g == 0)) | last

    @pl.when(jnp.logical_not(held_right))
    def _():
        to_right.start()

    @pl.when(jnp.logical_not(first | held_left))
    def _():
        to_left.start()

    for c in own_sibling:
        c.start()

    for there, copies in ((has_up, to_up), (has_down, to_down)):

        @pl.when(there)
        def _(copies=copies):
            copies[0].start()
            copies[2].start()

        @pl.when(there & jnp.logical_not(first))
        def _(copies=copies):
            copies[1].start()

    def step_out(n):
        for side in range(2):
            there = plane(2**n if side == 0 else PLANE - 2**n)
            pl.semaphore_signal(known.at[n, side], inc=1, device_id=there, device_id_type=MESH)

    def step_in(n):
        for side in range(2):
            pl.semaphore_wait(known.at[n, side], 1)

    def answer():
        for d in range(RING - 1, 0, -1):

            @pl.when(z < d)
            def _(d=d):
                pl.semaphore_wait(hello.at[d], 1)
                gather(RING - d).start()

    @pl.when(is_polar)
    def _():
        step_out(0)

    prepare_base()

    @pl.when(is_polar)
    def _():
        step_in(0)
        step_out(1)

    prepare_band()

    @pl.when(is_polar)
    def _():
        step_in(1)
        step_out(2)

    @pl.when(is_polar)
    def _():
        pl.when(z >= RING // 4)(answer)
        prepare_polar()
        pl.when(z < RING // 4)(answer)

    for c, d in zip(own_across, passed_on):
        c.wait_recv()
        d.start()

    for n, there, copy in ((0, first, to_left), (1, first & has_up, to_up[1]), (2, first & has_down, to_down[1])):

        @pl.when(there)
        def _(n=n, copy=copy):
            pl.semaphore_wait(seam.at[n], 1)
            copy.start()

    pl.when(held_right)(to_right.start)
    pl.when(held_left)(to_left.start)
    load_w.wait()
    for k in range(BASES):
        own_sibling[k].wait_recv()
        passed_on[k].wait_recv()
        hi, lo = split(wall[k])
        whi[CH * k : CH * k + CH, :] = hi
        wlo[CH * k : CH * k + CH, :] = lo

    def mix(taps):
        return dot3(split(taps), (whi[...], wlo[...]))

    def partial(n):
        d = distance(n)
        return remote(mixp.at[pl.ds(16 * n, 16)], rs.at[n], rsem_s, rsem_r, plane(d))

    def partials():
        rows = rs.at[pl.ds(0, PLANE - 1)]
        return remote(rows, rows, rsem_s, rsem_r, plane(1))

    @pl.when(is_polar)
    def _():
        for d in range(1, RING):
            gather(d).wait_recv()
        sources = split(xz[...].reshape(CH, CH))
        step_in(2)
        for half in range(2):
            rows = slice(128 * half, 128 * half + 128)
            taps = [dot3((chi[k, rows], clo[k, rows]), sources) for k in range(BASES)]
            mixp[rows] = mix(jnp.concatenate(taps, axis=1))
            for n in range(8 * half, min(8 * half + 8, PLANE - 1)):
                partial(n).start()

    to_right.wait_recv()
    to_left.wait_recv()
    sub = iota((8, CH), 0)

    @pl.when(has_up)
    def _():
        for c in to_down:
            c.wait_recv()
        lrecv[0] = jnp.where(sub < 4, corner[0], lrecv[0])
        rrecv[0] = jnp.where(sub < 4, corner[1], rrecv[0])

    @pl.when(jnp.logical_not(has_up))
    def _():
        xp[0:2] = jnp.zeros((2, COLS, CH), F32)

    @pl.when(has_down)
    def _():
        for c in to_up:
            c.wait_recv()
        lrecv[GROUPS - 1] = jnp.where(sub < 4, lrecv[GROUPS - 1], corner[2])
        rrecv[GROUPS - 1] = jnp.where(sub < 4, rrecv[GROUPS - 1], corner[3])

    @pl.when(jnp.logical_not(has_down))
    def _():
        xp[ROWS + 2 : ROWS + 4] = jnp.zeros((2, COLS, CH), F32)

    load_b.wait()
    shift = bias[...]
    empty = jnp.zeros((16, CH), F32)
    for s in range(TILES):
        x = jnp.concatenate(
            [
                xp[TILE * s : TILE * s + TILE + 4].reshape(160, CH),
                lrecv[4 * s : 4 * s + 5].reshape(40, CH),
                rrecv[4 * s : 4 * s + 5].reshape(40, CH),
                empty,
            ],
            axis=0,
        )
        tile = dot3(split(band[s]), split(x))
        mixed = mix(jnp.concatenate([tile[128 * k : 128 * k + 128] for k in range(BASES)], axis=1))
        out[TILE * s : TILE * s + TILE] = gelu(mixed + shift).reshape(TILE, COLS, CH)

    for c in own_across + own_sibling + passed_on + [to_left, to_right]:
        c.wait_send()

    @pl.when(has_up)
    def _():
        for c in to_up:
            c.wait_send()

    @pl.when(has_down)
    def _():
        for c in to_down:
            c.wait_send()

    @pl.when(is_polar)
    def _():
        for d in range(1, RING):
            gather(d).wait_send()
        partials().wait_send()

    @pl.when(is_polar)
    def _():
        total = mixp[16 * PLANE - 16 : 16 * PLANE, :]
        partials().wait_recv()
        for n in range(PLANE - 1):
            total = total + rs[n]
        total = gelu(total + shift)
        for p in range(2):
            out[p + south * (ROWS - 1 - 2 * p)] = total[8 * p : 8 * p + 8]


def on_device(atmosphere, disc_basis, polar_basis, widths, weights, channel_bias):
    anywhere = pl.BlockSpec(memory_space=pltpu.MemorySpace.HBM)

    def in_hbm(x):
        return pltpu.with_memory_space_constraint(x, pltpu.MemorySpace.HBM)


    def vmem(*shape, dtype=F32):
        return pltpu.VMEM(shape, dtype)

    dma = pltpu.SemaphoreType.DMA
    return pl.pallas_call(
        kernel,
        out_shape=pltpu.VMEM((ROWS, COLS, CH), F32),
        in_specs=[anywhere] * 6,
        out_specs=pl.BlockSpec(memory_space=pltpu.VMEM),
        scratch_shapes=[
            vmem(ROWS + 4, COLS, CH),
            vmem(GROUPS, 8, CH),
            vmem(GROUPS, 8, CH),
            vmem(GROUPS, 8, CH),
            vmem(GROUPS, 8, CH),
            vmem(4, 8, CH),
            vmem(5, 5, BASES, ROWS),
            vmem(BASES, 2, 4, 1024),
            vmem(1, ROWS, dtype=jnp.int32),
            vmem(1, CH),
            vmem(BASES, CH, CH),
            vmem(BASES * CH, CH, dtype=BF16),
            vmem(BASES * CH, CH, dtype=BF16),
            vmem(BASES, 128, 128),
            vmem(BASES, 128, 128),
            vmem(BASES, ROWS, 128),
            vmem(BASES, ROWS, 128),
            vmem(TILES, BASES * TILE * 8, 256),
            vmem(4, RING, 8, CH),
            vmem(24, 1024),
            vmem(2 * PLANE, 24, 128),
            vmem(2 * PLANE, 24, 128),
            vmem(BASES, 256, 256, dtype=BF16),
            vmem(BASES, 256, 256, dtype=BF16),
            vmem(256, CH),
            vmem(PLANE, 16, CH),
            dma((7,)),
            dma((8,)),
            dma((8,)),
            dma((BASES, 3)),
            dma((BASES, 3)),
            dma((RING,)),
            dma((RING,)),
            dma,
            dma,
            pltpu.SemaphoreType.REGULAR((3, 2)),
            pltpu.SemaphoreType.REGULAR((RING,)),
            pltpu.SemaphoreType.REGULAR,
            pltpu.SemaphoreType.REGULAR((3,)),
        ],
        compiler_params=pltpu.CompilerParams(
            collective_id=0, has_side_effects=True, vmem_limit_bytes=32 * 1024 * 1024
        ),
        name="disco",
    )(
        in_hbm(atmosphere),
        in_hbm(jnp.transpose(disc_basis, (2, 3, 0, 1))),
        in_hbm(polar_basis),
        in_hbm(widths.reshape(1, ROWS)),
        in_hbm(weights),
        in_hbm(channel_bias),
    )


def solution(mesh):
    return jax.shard_map(
        on_device,
        mesh=mesh,
        in_specs=(
            P("lat", "lon", None),
            P(None, "lat", None, None),
            P(),
            P("lat"),
            P(None, None, "lat", None),
            P(),
        ),
        out_specs=P("lat", "lon", None),
        check_vma=False,
    )
```

```python
import jax
import jax.numpy as jnp
from jax import lax
from jax.experimental import pallas as pl
from jax.experimental.pallas import tpu as pltpu
from jax.sharding import PartitionSpec as P

MESH = pl.DeviceIdType.MESH
F32 = jnp.float32
BF16 = jnp.bfloat16

ROWS, COLS, CH = 64, 8, 256
BASES = 3
TILE = 16
TILES = ROWS // TILE
GROUPS = (ROWS + 4) // 4
RING = 8
PLANE = 16
LON = RING * PLANE
LAT = 4


def split(x):
    hi = x.astype(BF16)
    return hi, (x - hi.astype(F32)).astype(BF16)


def dot3(a, b):
    def dot(x, y):
        return jnp.dot(x, y, preferred_element_type=F32)

    return dot(a[0], b[0]) + (dot(a[0], b[1]) + dot(a[1], b[0]))


def gelu(x):
    return 0.5 * x * (1.0 + lax.erf(x * 0.7071067811865476))


def iota(shape, dim):
    return lax.broadcasted_iota(jnp.int32, shape, dim)


def spread(ref, lead, row):
    return jnp.broadcast_to(ref[lead, pl.ds(row, 1), :], (8, 128))


def build_base(disc, wid, flip_main, flip_edge, main, edge):
    flip_main[...] = jnp.zeros_like(flip_main)
    flip_edge[...] = jnp.zeros_like(flip_edge)
    width = wid[...]
    for b in range(5):
        keep = (width >= abs(b - 2)).astype(F32)
        for k in range(BASES):
            for a in range(5):
                row = disc[a, b, k : k + 1, :] * keep
                at = (8 * a + b - 2) % 128
                flip_main[k, at : at + 1, 0:ROWS] = row
                if b < 2:
                    at = 32 + 2 * a + b
                    flip_edge[k, at : at + 1, 0:ROWS] = row
                if b > 2:
                    at = 65 + 2 * a + b - 3
                    flip_edge[k, at : at + 1, 0:ROWS] = row
    for k in range(BASES):
        main[k] = flip_main[k].T[0:ROWS]
        edge[k] = flip_edge[k].T[0:ROWS]


def build_band(main, edge, band):
    sub, lane = iota((8, 128), 0), iota((8, 128), 1)
    near = jnp.abs(lane % 8 - sub) <= 2
    side = ((sub < 2) & (lane < 64)) | ((sub >= 6) & (lane >= 64))
    odd = lane % 2 == 1
    fits = (sub == 0) | (sub == 7) | ((sub == 1) & odd) | ((sub == 6) & ~odd)
    low = lane < 32

    def step(n, carry):
        k, s = n // TILES, n % TILES
        for i in range(TILE):
            row = s * TILE + i
            m = pltpu.roll(spread(main, k, row), 8 * i, 1, stride=1, stride_axis=0)
            m = jnp.where(near, m, 0.0)
            h = jnp.where(side, spread(edge, k, row), 0.0)
            h = jnp.where(fits, pltpu.roll(h, 2 * i, 1, stride=1, stride_axis=0), 0.0)
            if i >= TILE - 4:
                h = jnp.where(low, m, h)
                m = jnp.where(low, 0.0, m)
            at = pl.multiple_of(k * TILE * 8, 8) + 8 * i
            band[s, pl.ds(at, 8), 0:128] = m
            band[s, pl.ds(at, 8), 128:256] = h
        return carry

    lax.fori_loop(0, BASES * TILES, step, 0)


def build_shifts(polar, rows, near, far, z):
    for k in range(BASES):
        for p in range(2):
            at = (2 * k + p) * 4
            rows[at : at + 4, :] = polar[k, p]
    lane = iota((24, 128), 1)
    parts = [rows[:, 128 * d : 128 * d + 128] for d in range(RING)]
    bits = [(lane // (8 * 2**b)) % 2 == 1 for b in range(3)]
    for b in range(3):
        turned = list(parts)
        for d in range(RING):
            if (d >> b) & 1 == 0:
                e = d + 2**b
                shift = 8 * 2**b
                turned[d] = jnp.where(bits[b], pltpu.roll(parts[e], shift, 1), parts[d])
                turned[e] = jnp.where(bits[b], parts[e], pltpu.roll(parts[d], 128 - shift, 1))
        parts = turned
    lower = lane < 64
    for t in range(PLANE):
        v = parts[t % 8]
        other = pltpu.roll(v, 64, 1)
        v = jnp.where(lower, v, other) if t < 8 else jnp.where(lower, other, v)
        here = pltpu.roll(v, 8 * z, 1)
        after = pltpu.roll(here, 8, 1)
        before = pltpu.roll(here, 120, 1)
        near[PLANE + t] = here
        near[t] = after
        far[PLANE + t] = before
        far[t] = here


def distance(n):
    return PLANE // 2 + (n + 1) // 2 * (1 - 2 * (n % 2))


def build_circular(near, far, chi, clo, g, south):
    sub, lane = iota((8, 128), 0), iota((8, 128), 1)
    over = lane % 8 + sub >= 8
    last = (lane // 8) % 8 == 7
    upper = (lane >= 64) ^ (last & over)

    def step(n, carry):
        at = PLANE + g - (g + distance(n)) % PLANE
        for k in range(BASES):
            for h in range(2):
                blocks = []
                for p in range(2):
                    first = (2 * k + p) * 4
                    q0 = first + 2 * h + south * (3 - 4 * h)
                    q1 = first + 2 * h + 1 + south * (1 - 4 * h)
                    a = jnp.where(upper, spread(near, at, q1), spread(near, at, q0))
                    b = jnp.where(upper, spread(far, at - 1, q1), spread(far, at - 1, q0))
                    v = jnp.where(over, b, a)
                    blocks.append(pltpu.roll(v, 0, 1, stride=1, stride_axis=0))
                rows = pl.ds(pl.multiple_of(n * 16, 16), 16)
                hi, lo = split(jnp.concatenate(blocks, axis=0))
                chi[k, rows, 128 * h : 128 * h + 128] = hi
                clo[k, rows, 128 * h : 128 * h + 128] = lo
        return carry

    lax.fori_loop(0, PLANE, step, 0)


def pack(xp, left, right):
    sub = iota((8, CH), 0)

    def place(rows, shifts):
        total = jnp.zeros((8, CH), F32)
        for r in range(4):
            if rows[r] is not None:
                moved = pltpu.roll(rows[r], shifts[r], 0) if shifts[r] else rows[r]
                total = jnp.where(sub // 2 == r, moved, total)
        return total

    def group(t, rows):
        left[t] = place(rows, (0, 2, 4, 6))
        right[t] = place(rows, (2, 4, 6, 0))

    group(0, [None, None, xp[2], xp[3]])
    group(GROUPS - 1, [xp[64], xp[65], None, None])

    def step(t, carry):
        group(t, [xp[4 * t + r] for r in range(4)])
        return carry

    lax.fori_loop(1, GROUPS - 1, step, 0)


def kernel(
    atm, disc_in, polar_in, wid_in, w_in, bias_in, out,
    xp, lsend, rsend, lrecv, rrecv, corner, disc, polar, wid, bias, wall, whi, wlo,
    flip_main, flip_edge, main, edge, band, xz, prow, shift_a, shift_b, chi, clo, mixp, rs,
    lsem, halo_s, halo_r, wsem_s, wsem_r, zsem_s, zsem_r, rsem_s, rsem_r, known, hello, near, seam,
):
    lat, lon = lax.axis_index("lat"), lax.axis_index("lon")
    z, g = lon // PLANE, lon % PLANE
    before, after = (lon + LON - 1) % LON, (lon + 1) % LON
    sibling = lat + 1 - 2 * (lat % 2)
    across = ((lat + 2) % LAT, lon + 1 - 2 * (lon % 2))
    south = lat // (LAT - 1)
    has_up, has_down = lat > 0, lat < LAT - 1
    first, last = lon == 0, lon == LON - 1
    is_polar = (lat == 0) | (lat == LAT - 1)
    up, down = jnp.maximum(lat - 1, 0), jnp.minimum(lat + 1, LAT - 1)

    def local(src, dst, n):
        return pltpu.make_async_copy(src, dst, lsem.at[n])

    source_row = south * (ROWS - 4)
    load_x = local(atm, xp.at[pl.ds(2, ROWS)], 0)
    load_w = local(w_in.at[0], wall.at[:, pl.ds(pl.multiple_of(64 * lat, 64), 64)], 1)
    load_d = local(disc_in, disc, 2)
    load_wid = local(wid_in, wid, 3)
    load_p = local(polar_in.at[south], polar, 4)
    load_b = local(bias_in, bias, 6)
    load_z = local(atm.at[pl.ds(source_row, 4)], xz.at[:, z], 5)

    def remote(src, dst, s, r, device):
        return pltpu.make_async_remote_copy(src, dst, s, r, device_id=device, device_id_type=MESH)

    def ring(d):
        return (lat, ((z + d) % RING) * PLANE + g)

    def plane(d):
        return (lat, z * PLANE + (g + d) % PLANE)

    barrier = pltpu.get_barrier_semaphore()

    def greet(device):
        pl.semaphore_signal(barrier, inc=1, device_id=device, device_id_type=MESH)

    late = z >= RING // 2
    turn = PLANE - 1 - 2 * g
    turning = is_polar & ((g == 0) | (g == PLANE - 1))

    even = lon % 2 == 0
    above, below = lat == LAT - 1, lat != LAT - 2
    neighbours = [
        (jnp.logical_not(last), even, (lat, after)),
        (jnp.logical_not(first), even, (lat, before)),
        (has_up, above, (up, lon)),
        (has_down, below, (down, lon)),
        (has_up & jnp.logical_not(last), above | ((lat == 2) & even), (up, after)),
        (has_down & jnp.logical_not(last), (lat == 0) | (below & even), (down, after)),
        (has_up & jnp.logical_not(first), above | ((lat == 2) & even), (up, before)),
        (has_down & jnp.logical_not(first), (lat == 0) | (below & even), (down, before)),
        (lat >= 0, is_polar, across),
        (turning, g == 0, (lat, lon + turn)),
    ]

    def count(*conditions):
        return sum(c.astype(jnp.int32) for c in conditions)

    @pl.when(is_polar)
    def _():
        load_z.start()

    for there, later, device in neighbours:

        @pl.when(there & later)
        def _(device=device):
            greet(device)

    for there, row in ((first, lat), (first & has_up, up), (first & has_down, down)):

        @pl.when(there)
        def _(row=row):
            greet((row, before))

    @pl.when(is_polar)
    def _():
        for d in range(1, RING):

            @pl.when(z + d < RING)
            def _(d=d):
                greet(ring(d))

    load_x.start()

    def prepare_base():
        load_d.wait()
        load_wid.wait()
        build_base(disc, wid, flip_main, flip_edge, main, edge)

    def prepare_band():
        build_band(main, edge, band)

    def prepare_polar():
        load_p.wait()
        build_shifts(polar, prow, shift_a, shift_b, z)
        build_circular(shift_a, shift_b, chi, clo, g, south)

    greeted = count(*[there & jnp.logical_not(later) for there, later, _ in neighbours])
    greeted += count(last, last & has_up, last & has_down) + z * count(is_polar)

    @pl.when(greeted > 0)
    def _():
        pl.semaphore_wait(barrier, greeted)

    def gather(d):
        return remote(xz.at[:, z], xz.at[:, z], zsem_s.at[d], zsem_r.at[d], ring(d))

    def shard(k, n, source_lat, device):
        rows = pl.ds(pl.multiple_of(64 * source_lat, 64), 64)
        source = wall.at[k, rows] if n == 2 else w_in.at[0, k]
        return remote(source, wall.at[k, rows], wsem_s.at[k, n], wsem_r.at[k, n], device)

    own_across = [shard(k, 0, lat, across) for k in range(BASES)]
    own_sibling = [shard(k, 1, lat, (sibling, lon)) for k in range(BASES)]
    passed_on = [shard(k, 2, (lat + 2) % LAT, (sibling, lon)) for k in range(BASES)]
    to_left = remote(lsend, rrecv, halo_s.at[0], halo_r.at[0], (lat, before))
    to_right = remote(rsend, lrecv, halo_s.at[1], halo_r.at[1], (lat, after))
    to_up = [
        remote(atm.at[pl.ds(0, 2)], xp.at[pl.ds(ROWS + 2, 2)], halo_s.at[2], halo_r.at[2], (up, lon)),
        remote(lsend.at[0], corner.at[3], halo_s.at[3], halo_r.at[3], (up, before)),
        remote(rsend.at[0], corner.at[2], halo_s.at[4], halo_r.at[4], (up, after)),
    ]
    to_down = [
        remote(atm.at[pl.ds(ROWS - 2, 2)], xp.at[pl.ds(0, 2)], halo_s.at[5], halo_r.at[5], (down, lon)),
        remote(lsend.at[GROUPS - 1], corner.at[1], halo_s.at[6], halo_r.at[6], (down, before)),
        remote(rsend.at[GROUPS - 1], corner.at[0], halo_s.at[7], halo_r.at[7], (down, after)),
    ]

    @pl.when(is_polar)
    def _():
        load_z.wait()
        for d in range(1, RING):

            @pl.when(z + d >= RING)
            def _(d=d):
                gather(d).start()

        for d in range(1, RING):

            @pl.when(z + d >= RING)
            def _(d=d):
                pl.semaphore_signal(hello.at[d], inc=1, device_id=ring(d), device_id_type=MESH)

    for there, later, device in neighbours:

        @pl.when(there & jnp.logical_not(later))
        def _(device=device):
            pl.semaphore_signal(near, inc=1, device_id=device, device_id_type=MESH)

    @pl.when(last)
    def _():
        pl.semaphore_signal(seam.at[0], inc=1, device_id=(lat, after), device_id_type=MESH)

    @pl.when(last & has_up)
    def _():
        pl.semaphore_signal(seam.at[2], inc=1, device_id=(up, after), device_id_type=MESH)

    @pl.when(last & has_down)
    def _():
        pl.semaphore_signal(seam.at[1], inc=1, device_id=(down, after), device_id_type=MESH)

    for c in (load_w, load_d, load_wid, load_b):
        c.start()

    pl.when(is_polar)(load_p.start)
    load_x.wait()
    pack(xp, lsend, rsend)
    to_come = count(*[there & later for there, later, _ in neighbours])

    @pl.when(to_come > 0)
    def _():
        pl.semaphore_wait(near, to_come)

    for c in own_across:
        c.start()

    held_right = late & (g == PLANE - 1) & jnp.logical_not(last)
    held_left = (late & (g == 0)) | last

    @pl.when(jnp.logical_not(held_right))
    def _():
        to_right.start()

    @pl.when(jnp.logical_not(first | held_left))
    def _():
        to_left.start()

    for c in own_sibling:
        c.start()

    for there, copies in ((has_up, to_up), (has_down, to_down)):

        @pl.when(there)
        def _(copies=copies):
            copies[0].start()
            copies[2].start()

        @pl.when(there & jnp.logical_not(first))
        def _(copies=copies):
            copies[1].start()

    def step_out(n):
        for side in range(2):
            there = plane(2**n if side == 0 else PLANE - 2**n)
            pl.semaphore_signal(known.at[n, side], inc=1, device_id=there, device_id_type=MESH)

    def step_in(n):
        for side in range(2):
            pl.semaphore_wait(known.at[n, side], 1)

    def answer():
        for d in range(RING - 1, 0, -1):

            @pl.when(z < d)
            def _(d=d):
                pl.semaphore_wait(hello.at[d], 1)
                gather(RING - d).start()

    @pl.when(is_polar)
    def _():
        step_out(0)

    prepare_base()

    @pl.when(is_polar)
    def _():
        step_in(0)
        step_out(1)

    prepare_band()

    @pl.when(is_polar)
    def _():
        step_in(1)
        step_out(2)

    @pl.when(is_polar)
    def _():
        pl.when(z >= RING // 4)(answer)
        prepare_polar()
        pl.when(z < RING // 4)(answer)

    for c, d in zip(own_across, passed_on):
        c.wait_recv()
        d.start()

    for n, there, copy in ((0, first, to_left), (1, first & has_up, to_up[1]), (2, first & has_down, to_down[1])):

        @pl.when(there)
        def _(n=n, copy=copy):
            pl.semaphore_wait(seam.at[n], 1)
            copy.start()

    pl.when(held_right)(to_right.start)
    pl.when(held_left)(to_left.start)
    load_w.wait()
    for k in range(BASES):
        own_sibling[k].wait_recv()
        passed_on[k].wait_recv()
        hi, lo = split(wall[k])
        whi[CH * k : CH * k + CH, :] = hi
        wlo[CH * k : CH * k + CH, :] = lo

    def mix(taps):
        return dot3(split(taps), (whi[...], wlo[...]))

    def partial(n):
        d = distance(n)
        return remote(mixp.at[pl.ds(16 * n, 16)], rs.at[n], rsem_s, rsem_r, plane(d))

    def partials():
        rows = rs.at[pl.ds(0, PLANE - 1)]
        return remote(rows, rows, rsem_s, rsem_r, plane(1))

    @pl.when(is_polar)
    def _():
        for d in range(1, RING):
            gather(d).wait_recv()
        sources = split(xz[...].reshape(CH, CH))
        step_in(2)
        for half in range(2):
            rows = slice(128 * half, 128 * half + 128)
            taps = [dot3((chi[k, rows], clo[k, rows]), sources) for k in range(BASES)]
            mixp[rows] = mix(jnp.concatenate(taps, axis=1))
            for n in range(8 * half, min(8 * half + 8, PLANE - 1)):
                partial(n).start()

    to_right.wait_recv()
    to_left.wait_recv()
    sub = iota((8, CH), 0)

    @pl.when(has_up)
    def _():
        for c in to_down:
            c.wait_recv()
        lrecv[0] = jnp.where(sub < 4, corner[0], lrecv[0])
        rrecv[0] = jnp.where(sub < 4, corner[1], rrecv[0])

    @pl.when(jnp.logical_not(has_up))
    def _():
        xp[0:2] = jnp.zeros((2, COLS, CH), F32)

    @pl.when(has_down)
    def _():
        for c in to_up:
            c.wait_recv()
        lrecv[GROUPS - 1] = jnp.where(sub < 4, lrecv[GROUPS - 1], corner[2])
        rrecv[GROUPS - 1] = jnp.where(sub < 4, rrecv[GROUPS - 1], corner[3])

    @pl.when(jnp.logical_not(has_down))
    def _():
        xp[ROWS + 2 : ROWS + 4] = jnp.zeros((2, COLS, CH), F32)

    load_b.wait()
    shift = bias[...]
    empty = jnp.zeros((16, CH), F32)
    for s in range(TILES):
        x = jnp.concatenate(
            [
                xp[TILE * s : TILE * s + TILE + 4].reshape(160, CH),
                lrecv[4 * s : 4 * s + 5].reshape(40, CH),
                rrecv[4 * s : 4 * s + 5].reshape(40, CH),
                empty,
            ],
            axis=0,
        )
        tile = dot3(split(band[s]), split(x))
        mixed = mix(jnp.concatenate([tile[128 * k : 128 * k + 128] for k in range(BASES)], axis=1))
        out[TILE * s : TILE * s + TILE] = gelu(mixed + shift).reshape(TILE, COLS, CH)

    for c in own_across + own_sibling + passed_on + [to_left, to_right]:
        c.wait_send()

    @pl.when(has_up)
    def _():
        for c in to_up:
            c.wait_send()

    @pl.when(has_down)
    def _():
        for c in to_down:
            c.wait_send()

    @pl.when(is_polar)
    def _():
        for d in range(1, RING):
            gather(d).wait_send()
        partials().wait_send()

    @pl.when(is_polar)
    def _():
        total = mixp[16 * PLANE - 16 : 16 * PLANE, :]
        partials().wait_recv()
        for n in range(PLANE - 1):
            total = total + rs[n]
        total = gelu(total + shift)
        for p in range(2):
            out[p + south * (ROWS - 1 - 2 * p)] = total[8 * p : 8 * p + 8]


def on_device(atmosphere, disc_basis, polar_basis, widths, weights, channel_bias):
    anywhere = pl.BlockSpec(memory_space=pltpu.MemorySpace.HBM)

    def in_hbm(x):
        return pltpu.with_memory_space_constraint(x, pltpu.MemorySpace.HBM)


    def vmem(*shape, dtype=F32):
        return pltpu.VMEM(shape, dtype)

    dma = pltpu.SemaphoreType.DMA
    return pl.pallas_call(
        kernel,
        out_shape=pltpu.VMEM((ROWS, COLS, CH), F32),
        in_specs=[anywhere] * 6,
        out_specs=pl.BlockSpec(memory_space=pltpu.VMEM),
        scratch_shapes=[
            vmem(ROWS + 4, COLS, CH),
            vmem(GROUPS, 8, CH),
            vmem(GROUPS, 8, CH),
            vmem(GROUPS, 8, CH),
            vmem(GROUPS, 8, CH),
            vmem(4, 8, CH),
            vmem(5, 5, BASES, ROWS),
            vmem(BASES, 2, 4, 1024),
            vmem(1, ROWS, dtype=jnp.int32),
            vmem(1, CH),
            vmem(BASES, CH, CH),
            vmem(BASES * CH, CH, dtype=BF16),
            vmem(BASES * CH, CH, dtype=BF16),
            vmem(BASES, 128, 128),
            vmem(BASES, 128, 128),
            vmem(BASES, ROWS, 128),
            vmem(BASES, ROWS, 128),
            vmem(TILES, BASES * TILE * 8, 256),
            vmem(4, RING, 8, CH),
            vmem(24, 1024),
            vmem(2 * PLANE, 24, 128),
            vmem(2 * PLANE, 24, 128),
            vmem(BASES, 256, 256, dtype=BF16),
            vmem(BASES, 256, 256, dtype=BF16),
            vmem(256, CH),
            vmem(PLANE, 16, CH),
            dma((7,)),
            dma((8,)),
            dma((8,)),
            dma((BASES, 3)),
            dma((BASES, 3)),
            dma((RING,)),
            dma((RING,)),
            dma,
            dma,
            pltpu.SemaphoreType.REGULAR((3, 2)),
            pltpu.SemaphoreType.REGULAR((RING,)),
            pltpu.SemaphoreType.REGULAR,
            pltpu.SemaphoreType.REGULAR((3,)),
        ],
        compiler_params=pltpu.CompilerParams(
            collective_id=0, has_side_effects=True, vmem_limit_bytes=32 * 1024 * 1024
        ),
        name="disco",
    )(
        in_hbm(atmosphere),
        in_hbm(jnp.transpose(disc_basis, (2, 3, 0, 1))),
        in_hbm(polar_basis),
        in_hbm(widths.reshape(1, ROWS)),
        in_hbm(weights),
        in_hbm(channel_bias),
    )


def solution(mesh):
    return jax.shard_map(
        on_device,
        mesh=mesh,
        in_specs=(
            P("lat", "lon", None),
            P(None, "lat", None, None),
            P(),
            P("lat"),
            P(None, None, "lat", None),
            P(),
        ),
        out_specs=P("lat", "lon", None),
        check_vma=False,
    )
```

```python
import jax
import jax.numpy as jnp
from jax import lax
from jax.experimental import pallas as pl
from jax.experimental.pallas import tpu as pltpu
from jax.sharding import PartitionSpec as P

MESH = pl.DeviceIdType.MESH
F32 = jnp.float32
BF16 = jnp.bfloat16

ROWS, COLS, CH = 64, 8, 256
BASES = 3
TILE = 16
TILES = ROWS // TILE
GROUPS = (ROWS + 4) // 4
RING = 8
PLANE = 16
LON = RING * PLANE
LAT = 4


def split(x):
    hi = x.astype(BF16)
    return hi, (x - hi.astype(F32)).astype(BF16)


def dot3(a, b):
    def dot(x, y):
        return jnp.dot(x, y, preferred_element_type=F32)

    return dot(a[0], b[0]) + (dot(a[0], b[1]) + dot(a[1], b[0]))


def gelu(x):
    return 0.5 * x * (1.0 + lax.erf(x * 0.7071067811865476))


def iota(shape, dim):
    return lax.broadcasted_iota(jnp.int32, shape, dim)


def spread(ref, lead, row):
    return jnp.broadcast_to(ref[lead, pl.ds(row, 1), :], (8, 128))


def build_base(disc, wid, flip_main, flip_edge, main, edge):
    flip_main[...] = jnp.zeros_like(flip_main)
    flip_edge[...] = jnp.zeros_like(flip_edge)
    width = wid[...]
    for b in range(5):
        keep = (width >= abs(b - 2)).astype(F32)
        for k in range(BASES):
            for a in range(5):
                row = disc[a, b, k : k + 1, :] * keep
                at = (8 * a + b - 2) % 128
                flip_main[k, at : at + 1, 0:ROWS] = row
                if b < 2:
                    at = 32 + 2 * a + b
                    flip_edge[k, at : at + 1, 0:ROWS] = row
                if b > 2:
                    at = 65 + 2 * a + b - 3
                    flip_edge[k, at : at + 1, 0:ROWS] = row
    for k in range(BASES):
        main[k] = flip_main[k].T[0:ROWS]
        edge[k] = flip_edge[k].T[0:ROWS]


def build_band(main, edge, band):
    sub, lane = iota((8, 128), 0), iota((8, 128), 1)
    near = jnp.abs(lane % 8 - sub) <= 2
    side = ((sub < 2) & (lane < 64)) | ((sub >= 6) & (lane >= 64))
    odd = lane % 2 == 1
    fits = (sub == 0) | (sub == 7) | ((sub == 1) & odd) | ((sub == 6) & ~odd)
    low = lane < 32

    def step(n, carry):
        k, s = n // TILES, n % TILES
        for i in range(TILE):
            row = s * TILE + i
            m = pltpu.roll(spread(main, k, row), 8 * i, 1, stride=1, stride_axis=0)
            m = jnp.where(near, m, 0.0)
            h = jnp.where(side, spread(edge, k, row), 0.0)
            h = jnp.where(fits, pltpu.roll(h, 2 * i, 1, stride=1, stride_axis=0), 0.0)
            if i >= TILE - 4:
                h = jnp.where(low, m, h)
                m = jnp.where(low, 0.0, m)
            at = pl.multiple_of(k * TILE * 8, 8) + 8 * i
            band[s, pl.ds(at, 8), 0:128] = m
            band[s, pl.ds(at, 8), 128:256] = h
        return carry

    lax.fori_loop(0, BASES * TILES, step, 0)


def build_shifts(polar, rows, near, far, z):
    for k in range(BASES):
        for p in range(2):
            at = (2 * k + p) * 4
            rows[at : at + 4, :] = polar[k, p]
    lane = iota((24, 128), 1)
    parts = [rows[:, 128 * d : 128 * d + 128] for d in range(RING)]
    bits = [(lane // (8 * 2**b)) % 2 == 1 for b in range(3)]
    for b in range(3):
        turned = list(parts)
        for d in range(RING):
            if (d >> b) & 1 == 0:
                e = d + 2**b
                shift = 8 * 2**b
                turned[d] = jnp.where(bits[b], pltpu.roll(parts[e], shift, 1), parts[d])
                turned[e] = jnp.where(bits[b], parts[e], pltpu.roll(parts[d], 128 - shift, 1))
        parts = turned
    lower = lane < 64
    for t in range(PLANE):
        v = parts[t % 8]
        other = pltpu.roll(v, 64, 1)
        v = jnp.where(lower, v, other) if t < 8 else jnp.where(lower, other, v)
        here = pltpu.roll(v, 8 * z, 1)
        after = pltpu.roll(here, 8, 1)
        before = pltpu.roll(here, 120, 1)
        near[PLANE + t] = here
        near[t] = after
        far[PLANE + t] = before
        far[t] = here


def distance(n):
    return PLANE // 2 + (n + 1) // 2 * (1 - 2 * (n % 2))


def build_circular(near, far, chi, clo, g, south):
    sub, lane = iota((8, 128), 0), iota((8, 128), 1)
    over = lane % 8 + sub >= 8
    last = (lane // 8) % 8 == 7
    upper = (lane >= 64) ^ (last & over)

    def step(n, carry):
        at = PLANE + g - (g + distance(n)) % PLANE
        for k in range(BASES):
            for h in range(2):
                blocks = []
                for p in range(2):
                    first = (2 * k + p) * 4
                    q0 = first + 2 * h + south * (3 - 4 * h)
                    q1 = first + 2 * h + 1 + south * (1 - 4 * h)
                    a = jnp.where(upper, spread(near, at, q1), spread(near, at, q0))
                    b = jnp.where(upper, spread(far, at - 1, q1), spread(far, at - 1, q0))
                    v = jnp.where(over, b, a)
                    blocks.append(pltpu.roll(v, 0, 1, stride=1, stride_axis=0))
                rows = pl.ds(pl.multiple_of(n * 16, 16), 16)
                hi, lo = split(jnp.concatenate(blocks, axis=0))
                chi[k, rows, 128 * h : 128 * h + 128] = hi
                clo[k, rows, 128 * h : 128 * h + 128] = lo
        return carry

    lax.fori_loop(0, PLANE, step, 0)


def pack(xp, left, right):
    sub = iota((8, CH), 0)

    def place(rows, shifts):
        total = jnp.zeros((8, CH), F32)
        for r in range(4):
            if rows[r] is not None:
                moved = pltpu.roll(rows[r], shifts[r], 0) if shifts[r] else rows[r]
                total = jnp.where(sub // 2 == r, moved, total)
        return total

    def group(t, rows):
        left[t] = place(rows, (0, 2, 4, 6))
        right[t] = place(rows, (2, 4, 6, 0))

    group(0, [None, None, xp[2], xp[3]])
    group(GROUPS - 1, [xp[64], xp[65], None, None])

    def step(t, carry):
        group(t, [xp[4 * t + r] for r in range(4)])
        return carry

    lax.fori_loop(1, GROUPS - 1, step, 0)


def kernel(
    atm, disc_in, polar_in, wid_in, w_in, bias_in, out,
    xp, lsend, rsend, lrecv, rrecv, corner, disc, polar, wid, bias, wall, whi, wlo,
    flip_main, flip_edge, main, edge, band, xz, prow, shift_a, shift_b, chi, clo, mixp, rs,
    lsem, halo_s, halo_r, wsem_s, wsem_r, zsem_s, zsem_r, rsem_s, rsem_r, known, hello, near, seam,
):
    lat, lon = lax.axis_index("lat"), lax.axis_index("lon")
    z, g = lon // PLANE, lon % PLANE
    before, after = (lon + LON - 1) % LON, (lon + 1) % LON
    sibling = lat + 1 - 2 * (lat % 2)
    across = ((lat + 2) % LAT, lon + 1 - 2 * (lon % 2))
    south = lat // (LAT - 1)
    has_up, has_down = lat > 0, lat < LAT - 1
    first, last = lon == 0, lon == LON - 1
    is_polar = (lat == 0) | (lat == LAT - 1)
    up, down = jnp.maximum(lat - 1, 0), jnp.minimum(lat + 1, LAT - 1)

    def local(src, dst, n):
        return pltpu.make_async_copy(src, dst, lsem.at[n])

    source_row = south * (ROWS - 4)
    load_x = local(atm, xp.at[pl.ds(2, ROWS)], 0)
    load_w = local(w_in.at[0], wall.at[:, pl.ds(pl.multiple_of(64 * lat, 64), 64)], 1)
    load_d = local(disc_in, disc, 2)
    load_wid = local(wid_in, wid, 3)
    load_p = local(polar_in.at[south], polar, 4)
    load_b = local(bias_in, bias, 6)
    load_z = local(atm.at[pl.ds(source_row, 4)], xz.at[:, z], 5)

    def remote(src, dst, s, r, device):
        return pltpu.make_async_remote_copy(src, dst, s, r, device_id=device, device_id_type=MESH)

    def ring(d):
        return (lat, ((z + d) % RING) * PLANE + g)

    def plane(d):
        return (lat, z * PLANE + (g + d) % PLANE)

    barrier = pltpu.get_barrier_semaphore()

    def greet(device):
        pl.semaphore_signal(barrier, inc=1, device_id=device, device_id_type=MESH)

    late = z >= RING // 2
    turn = PLANE - 1 - 2 * g
    turning = is_polar & ((g == 0) | (g == PLANE - 1))

    even = lon % 2 == 0
    above, below = lat == LAT - 1, lat != LAT - 2
    neighbours = [
        (jnp.logical_not(last), even, (lat, after)),
        (jnp.logical_not(first), even, (lat, before)),
        (has_up, above, (up, lon)),
        (has_down, below, (down, lon)),
        (has_up & jnp.logical_not(last), above | ((lat == 2) & even), (up, after)),
        (has_down & jnp.logical_not(last), (lat == 0) | (below & even), (down, after)),
        (has_up & jnp.logical_not(first), above | ((lat == 2) & even), (up, before)),
        (has_down & jnp.logical_not(first), (lat == 0) | (below & even), (down, before)),
        (lat >= 0, is_polar, across),
        (turning, g == 0, (lat, lon + turn)),
    ]

    def count(*conditions):
        return sum(c.astype(jnp.int32) for c in conditions)

    @pl.when(is_polar)
    def _():
        load_z.start()

    for there, later, device in neighbours:

        @pl.when(there & later)
        def _(device=device):
            greet(device)

    for there, row in ((first, lat), (first & has_up, up), (first & has_down, down)):

        @pl.when(there)
        def _(row=row):
            greet((row, before))

    @pl.when(is_polar)
    def _():
        for d in range(1, RING):

            @pl.when(z + d < RING)
            def _(d=d):
                greet(ring(d))

    load_x.start()

    def prepare_base():
        load_d.wait()
        load_wid.wait()
        build_base(disc, wid, flip_main, flip_edge, main, edge)

    def prepare_band():
        build_band(main, edge, band)

    def prepare_polar():
        load_p.wait()
        build_shifts(polar, prow, shift_a, shift_b, z)
        build_circular(shift_a, shift_b, chi, clo, g, south)

    greeted = count(*[there & jnp.logical_not(later) for there, later, _ in neighbours])
    greeted += count(last, last & has_up, last & has_down) + z * count(is_polar)

    @pl.when(greeted > 0)
    def _():
        pl.semaphore_wait(barrier, greeted)

    def gather(d):
        return remote(xz.at[:, z], xz.at[:, z], zsem_s.at[d], zsem_r, ring(d))

    def shard(k, n, source_lat, device):
        rows = pl.ds(pl.multiple_of(64 * source_lat, 64), 64)
        source = wall.at[k, rows] if n == 2 else w_in.at[0, k]
        return remote(source, wall.at[k, rows], wsem_s.at[k, n], wsem_r.at[k, n], device)

    own_across = [shard(k, 0, lat, across) for k in range(BASES)]
    own_sibling = [shard(k, 1, lat, (sibling, lon)) for k in range(BASES)]
    passed_on = [shard(k, 2, (lat + 2) % LAT, (sibling, lon)) for k in range(BASES)]
    to_left = remote(lsend, rrecv, halo_s.at[0], halo_r.at[0], (lat, before))
    to_right = remote(rsend, lrecv, halo_s.at[1], halo_r.at[1], (lat, after))
    to_up = [
        remote(atm.at[pl.ds(0, 2)], xp.at[pl.ds(ROWS + 2, 2)], halo_s.at[2], halo_r.at[2], (up, lon)),
        remote(lsend.at[0], corner.at[3], halo_s.at[3], halo_r.at[3], (up, before)),
        remote(rsend.at[0], corner.at[2], halo_s.at[4], halo_r.at[4], (up, after)),
    ]
    to_down = [
        remote(atm.at[pl.ds(ROWS - 2, 2)], xp.at[pl.ds(0, 2)], halo_s.at[5], halo_r.at[5], (down, lon)),
        remote(lsend.at[GROUPS - 1], corner.at[1], halo_s.at[6], halo_r.at[6], (down, before)),
        remote(rsend.at[GROUPS - 1], corner.at[0], halo_s.at[7], halo_r.at[7], (down, after)),
    ]

    @pl.when(is_polar)
    def _():
        load_z.wait()
        for d in range(1, RING):

            @pl.when(z + d >= RING)
            def _(d=d):
                gather(d).start()

        for d in range(1, RING):

            @pl.when(z + d >= RING)
            def _(d=d):
                pl.semaphore_signal(hello.at[d], inc=1, device_id=ring(d), device_id_type=MESH)

    for there, later, device in neighbours:

        @pl.when(there & jnp.logical_not(later))
        def _(device=device):
            pl.semaphore_signal(near, inc=1, device_id=device, device_id_type=MESH)

    @pl.when(last)
    def _():
        pl.semaphore_signal(seam.at[0], inc=1, device_id=(lat, after), device_id_type=MESH)

    @pl.when(last & has_up)
    def _():
        pl.semaphore_signal(seam.at[2], inc=1, device_id=(up, after), device_id_type=MESH)

    @pl.when(last & has_down)
    def _():
        pl.semaphore_signal(seam.at[1], inc=1, device_id=(down, after), device_id_type=MESH)

    for c in (load_w, load_d, load_wid, load_b):
        c.start()

    pl.when(is_polar)(load_p.start)
    load_x.wait()
    pack(xp, lsend, rsend)
    to_come = count(*[there & later for there, later, _ in neighbours])

    @pl.when(to_come > 0)
    def _():
        pl.semaphore_wait(near, to_come)

    for c in own_across:
        c.start()

    held_right = late & (g == PLANE - 1) & jnp.logical_not(last)
    held_left = (late & (g == 0)) | last

    @pl.when(jnp.logical_not(held_right))
    def _():
        to_right.start()

    @pl.when(jnp.logical_not(first | held_left))
    def _():
        to_left.start()

    for c in own_sibling:
        c.start()

    for there, copies in ((has_up, to_up), (has_down, to_down)):

        @pl.when(there)
        def _(copies=copies):
            copies[0].start()
            copies[2].start()

        @pl.when(there & jnp.logical_not(first))
        def _(copies=copies):
            copies[1].start()

    def step_out(n):
        for side in range(2):
            there = plane(2**n if side == 0 else PLANE - 2**n)
            pl.semaphore_signal(known.at[n, side], inc=1, device_id=there, device_id_type=MESH)

    def step_in(n):
        for side in range(2):
            pl.semaphore_wait(known.at[n, side], 1)

    def answer():
        for d in range(RING - 1, 0, -1):

            @pl.when(z < d)
            def _(d=d):
                pl.semaphore_wait(hello.at[d], 1)
                gather(RING - d).start()

    @pl.when(is_polar)
    def _():
        step_out(0)

    prepare_base()

    @pl.when(is_polar)
    def _():
        step_in(0)
        step_out(1)

    prepare_band()

    @pl.when(is_polar)
    def _():
        step_in(1)
        step_out(2)

    @pl.when(is_polar)
    def _():
        pl.when(z >= RING // 4)(answer)
        prepare_polar()
        pl.when(z < RING // 4)(answer)

    for c, d in zip(own_across, passed_on):
        c.wait_recv()
        d.start()

    for n, there, copy in ((0, first, to_left), (1, first & has_up, to_up[1]), (2, first & has_down, to_down[1])):

        @pl.when(there)
        def _(n=n, copy=copy):
            pl.semaphore_wait(seam.at[n], 1)
            copy.start()

    pl.when(held_right)(to_right.start)
    pl.when(held_left)(to_left.start)
    load_w.wait()
    for k in range(BASES):
        own_sibling[k].wait_recv()
        passed_on[k].wait_recv()
        hi, lo = split(wall[k])
        whi[CH * k : CH * k + CH, :] = hi
        wlo[CH * k : CH * k + CH, :] = lo

    def mix(taps):
        return dot3(split(taps), (whi[...], wlo[...]))

    def partial(n):
        d = distance(n)
        return remote(mixp.at[pl.ds(16 * n, 16)], rs.at[n], rsem_s, rsem_r, plane(d))

    def partials():
        rows = rs.at[pl.ds(0, PLANE - 1)]
        return remote(rows, rows, rsem_s, rsem_r, plane(1))

    @pl.when(is_polar)
    def _():
        rows = xz.at[:, pl.ds(0, RING - 1)]
        remote(rows, rows, zsem_s.at[0], zsem_r, ring(1)).wait_recv()
        sources = split(xz[...].reshape(CH, CH))
        step_in(2)
        for half in range(2):
            rows = slice(128 * half, 128 * half + 128)
            taps = [dot3((chi[k, rows], clo[k, rows]), sources) for k in range(BASES)]
            mixp[rows] = mix(jnp.concatenate(taps, axis=1))
            for n in range(8 * half, min(8 * half + 8, PLANE - 1)):
                partial(n).start()

    to_right.wait_recv()
    to_left.wait_recv()
    sub = iota((8, CH), 0)

    @pl.when(has_up)
    def _():
        for c in to_down:
            c.wait_recv()
        lrecv[0] = jnp.where(sub < 4, corner[0], lrecv[0])
        rrecv[0] = jnp.where(sub < 4, corner[1], rrecv[0])

    @pl.when(jnp.logical_not(has_up))
    def _():
        xp[0:2] = jnp.zeros((2, COLS, CH), F32)

    @pl.when(has_down)
    def _():
        for c in to_up:
            c.wait_recv()
        lrecv[GROUPS - 1] = jnp.where(sub < 4, lrecv[GROUPS - 1], corner[2])
        rrecv[GROUPS - 1] = jnp.where(sub < 4, rrecv[GROUPS - 1], corner[3])

    @pl.when(jnp.logical_not(has_down))
    def _():
        xp[ROWS + 2 : ROWS + 4] = jnp.zeros((2, COLS, CH), F32)

    load_b.wait()
    shift = bias[...]
    empty = jnp.zeros((16, CH), F32)
    for s in range(TILES):
        x = jnp.concatenate(
            [
                xp[TILE * s : TILE * s + TILE + 4].reshape(160, CH),
                lrecv[4 * s : 4 * s + 5].reshape(40, CH),
                rrecv[4 * s : 4 * s + 5].reshape(40, CH),
                empty,
            ],
            axis=0,
        )
        tile = dot3(split(band[s]), split(x))
        mixed = mix(jnp.concatenate([tile[128 * k : 128 * k + 128] for k in range(BASES)], axis=1))
        out[TILE * s : TILE * s + TILE] = gelu(mixed + shift).reshape(TILE, COLS, CH)

    for c in own_across + own_sibling + passed_on + [to_left, to_right]:
        c.wait_send()

    @pl.when(has_up)
    def _():
        for c in to_up:
            c.wait_send()

    @pl.when(has_down)
    def _():
        for c in to_down:
            c.wait_send()

    @pl.when(is_polar)
    def _():
        for d in range(1, RING):
            gather(d).wait_send()
        partials().wait_send()

    @pl.when(is_polar)
    def _():
        total = mixp[16 * PLANE - 16 : 16 * PLANE, :]
        partials().wait_recv()
        for n in range(PLANE - 1):
            total = total + rs[n]
        total = gelu(total + shift)
        for p in range(2):
            out[p + south * (ROWS - 1 - 2 * p)] = total[8 * p : 8 * p + 8]


def on_device(atmosphere, disc_basis, polar_basis, widths, weights, channel_bias):
    anywhere = pl.BlockSpec(memory_space=pltpu.MemorySpace.HBM)

    def in_hbm(x):
        return pltpu.with_memory_space_constraint(x, pltpu.MemorySpace.HBM)


    def vmem(*shape, dtype=F32):
        return pltpu.VMEM(shape, dtype)

    dma = pltpu.SemaphoreType.DMA
    return pl.pallas_call(
        kernel,
        out_shape=pltpu.VMEM((ROWS, COLS, CH), F32),
        in_specs=[anywhere] * 6,
        out_specs=pl.BlockSpec(memory_space=pltpu.VMEM),
        scratch_shapes=[
            vmem(ROWS + 4, COLS, CH),
            vmem(GROUPS, 8, CH),
            vmem(GROUPS, 8, CH),
            vmem(GROUPS, 8, CH),
            vmem(GROUPS, 8, CH),
            vmem(4, 8, CH),
            vmem(5, 5, BASES, ROWS),
            vmem(BASES, 2, 4, 1024),
            vmem(1, ROWS, dtype=jnp.int32),
            vmem(1, CH),
            vmem(BASES, CH, CH),
            vmem(BASES * CH, CH, dtype=BF16),
            vmem(BASES * CH, CH, dtype=BF16),
            vmem(BASES, 128, 128),
            vmem(BASES, 128, 128),
            vmem(BASES, ROWS, 128),
            vmem(BASES, ROWS, 128),
            vmem(TILES, BASES * TILE * 8, 256),
            vmem(4, RING, 8, CH),
            vmem(24, 1024),
            vmem(2 * PLANE, 24, 128),
            vmem(2 * PLANE, 24, 128),
            vmem(BASES, 256, 256, dtype=BF16),
            vmem(BASES, 256, 256, dtype=BF16),
            vmem(256, CH),
            vmem(PLANE, 16, CH),
            dma((7,)),
            dma((8,)),
            dma((8,)),
            dma((BASES, 3)),
            dma((BASES, 3)),
            dma((RING,)),
            dma,
            dma,
            dma,
            pltpu.SemaphoreType.REGULAR((3, 2)),
            pltpu.SemaphoreType.REGULAR((RING,)),
            pltpu.SemaphoreType.REGULAR,
            pltpu.SemaphoreType.REGULAR((3,)),
        ],
        compiler_params=pltpu.CompilerParams(
            collective_id=0, has_side_effects=True, vmem_limit_bytes=32 * 1024 * 1024
        ),
        name="disco",
    )(
        in_hbm(atmosphere),
        in_hbm(jnp.transpose(disc_basis, (2, 3, 0, 1))),
        in_hbm(polar_basis),
        in_hbm(widths.reshape(1, ROWS)),
        in_hbm(weights),
        in_hbm(channel_bias),
    )


def solution(mesh):
    return jax.shard_map(
        on_device,
        mesh=mesh,
        in_specs=(
            P("lat", "lon", None),
            P(None, "lat", None, None),
            P(),
            P("lat"),
            P(None, None, "lat", None),
            P(),
        ),
        out_specs=P("lat", "lon", None),
        check_vma=False,
    )
```

```python
import jax
import jax.numpy as jnp
from jax import lax
from jax.experimental import pallas as pl
from jax.experimental.pallas import tpu as pltpu
from jax.sharding import PartitionSpec as P

MESH = pl.DeviceIdType.MESH
F32 = jnp.float32
BF16 = jnp.bfloat16

ROWS, COLS, CH = 64, 8, 256
BASES = 3
TILE = 16
TILES = ROWS // TILE
GROUPS = (ROWS + 4) // 4
RING = 8
PLANE = 16
LON = RING * PLANE
LAT = 4


def split(x):
    hi = x.astype(BF16)
    return hi, (x - hi.astype(F32)).astype(BF16)


def dot3(a, b):
    def dot(x, y):
        return jnp.dot(x, y, preferred_element_type=F32)

    return dot(a[0], b[0]) + (dot(a[0], b[1]) + dot(a[1], b[0]))


def gelu(x):
    return 0.5 * x * (1.0 + lax.erf(x * 0.7071067811865476))


def iota(shape, dim):
    return lax.broadcasted_iota(jnp.int32, shape, dim)


def spread(ref, lead, row):
    return jnp.broadcast_to(ref[lead, pl.ds(row, 1), :], (8, 128))


def build_base(disc, wid, flip_main, flip_edge, main, edge):
    flip_main[...] = jnp.zeros_like(flip_main)
    flip_edge[...] = jnp.zeros_like(flip_edge)
    width = wid[...]
    for b in range(5):
        keep = (width >= abs(b - 2)).astype(F32)
        for k in range(BASES):
            for a in range(5):
                row = disc[a, b, k : k + 1, :] * keep
                at = (8 * a + b - 2) % 128
                flip_main[k, at : at + 1, 0:ROWS] = row
                if b < 2:
                    at = 32 + 2 * a + b
                    flip_edge[k, at : at + 1, 0:ROWS] = row
                if b > 2:
                    at = 65 + 2 * a + b - 3
                    flip_edge[k, at : at + 1, 0:ROWS] = row
    for k in range(BASES):
        main[k] = flip_main[k].T[0:ROWS]
        edge[k] = flip_edge[k].T[0:ROWS]


def build_band(main, edge, band):
    sub, lane = iota((8, 128), 0), iota((8, 128), 1)
    near = jnp.abs(lane % 8 - sub) <= 2
    side = ((sub < 2) & (lane < 64)) | ((sub >= 6) & (lane >= 64))
    odd = lane % 2 == 1
    fits = (sub == 0) | (sub == 7) | ((sub == 1) & odd) | ((sub == 6) & ~odd)
    low = lane < 32

    def step(n, carry):
        k, s = n // TILES, n % TILES
        for i in range(TILE):
            row = s * TILE + i
            m = pltpu.roll(spread(main, k, row), 8 * i, 1, stride=1, stride_axis=0)
            m = jnp.where(near, m, 0.0)
            h = jnp.where(side, spread(edge, k, row), 0.0)
            h = jnp.where(fits, pltpu.roll(h, 2 * i, 1, stride=1, stride_axis=0), 0.0)
            if i >= TILE - 4:
                h = jnp.where(low, m, h)
                m = jnp.where(low, 0.0, m)
            at = pl.multiple_of(k * TILE * 8, 8) + 8 * i
            band[s, pl.ds(at, 8), 0:128] = m
            band[s, pl.ds(at, 8), 128:256] = h
        return carry

    lax.fori_loop(0, BASES * TILES, step, 0)


def build_shifts(polar, rows, near, far, z):
    for k in range(BASES):
        for p in range(2):
            at = (2 * k + p) * 4
            rows[at : at + 4, :] = polar[k, p]
    lane = iota((24, 128), 1)
    parts = [rows[:, 128 * d : 128 * d + 128] for d in range(RING)]
    bits = [(lane // (8 * 2**b)) % 2 == 1 for b in range(3)]
    for b in range(3):
        turned = list(parts)
        for d in range(RING):
            if (d >> b) & 1 == 0:
                e = d + 2**b
                shift = 8 * 2**b
                turned[d] = jnp.where(bits[b], pltpu.roll(parts[e], shift, 1), parts[d])
                turned[e] = jnp.where(bits[b], parts[e], pltpu.roll(parts[d], 128 - shift, 1))
        parts = turned
    lower = lane < 64
    for t in range(PLANE):
        v = parts[t % 8]
        other = pltpu.roll(v, 64, 1)
        v = jnp.where(lower, v, other) if t < 8 else jnp.where(lower, other, v)
        here = pltpu.roll(v, 8 * z, 1)
        after = pltpu.roll(here, 8, 1)
        before = pltpu.roll(here, 120, 1)
        near[PLANE + t] = here
        near[t] = after
        far[PLANE + t] = before
        far[t] = here


def distance(n):
    return PLANE // 2 + (n + 1) // 2 * (1 - 2 * (n % 2))


def build_circular(near, far, chi, clo, g, south):
    sub, lane = iota((8, 128), 0), iota((8, 128), 1)
    over = lane % 8 + sub >= 8
    last = (lane // 8) % 8 == 7
    upper = (lane >= 64) ^ (last & over)

    def step(n, carry):
        at = PLANE + g - (g + distance(n)) % PLANE
        for k in range(BASES):
            for h in range(2):
                blocks = []
                for p in range(2):
                    first = (2 * k + p) * 4
                    q0 = first + 2 * h + south * (3 - 4 * h)
                    q1 = first + 2 * h + 1 + south * (1 - 4 * h)
                    a = jnp.where(upper, spread(near, at, q1), spread(near, at, q0))
                    b = jnp.where(upper, spread(far, at - 1, q1), spread(far, at - 1, q0))
                    v = jnp.where(over, b, a)
                    blocks.append(pltpu.roll(v, 0, 1, stride=1, stride_axis=0))
                rows = pl.ds(pl.multiple_of(n * 16, 16), 16)
                hi, lo = split(jnp.concatenate(blocks, axis=0))
                chi[k, rows, 128 * h : 128 * h + 128] = hi
                clo[k, rows, 128 * h : 128 * h + 128] = lo
        return carry

    lax.fori_loop(0, PLANE, step, 0)


def pack(xp, left, right):
    sub = iota((8, CH), 0)

    def place(rows, shifts):
        total = jnp.zeros((8, CH), F32)
        for r in range(4):
            if rows[r] is not None:
                moved = pltpu.roll(rows[r], shifts[r], 0) if shifts[r] else rows[r]
                total = jnp.where(sub // 2 == r, moved, total)
        return total

    def group(t, rows):
        left[t] = place(rows, (0, 2, 4, 6))
        right[t] = place(rows, (2, 4, 6, 0))

    group(0, [None, None, xp[2], xp[3]])
    group(GROUPS - 1, [xp[64], xp[65], None, None])

    def step(t, carry):
        group(t, [xp[4 * t + r] for r in range(4)])
        return carry

    lax.fori_loop(1, GROUPS - 1, step, 0)


def kernel(
    atm, disc_in, polar_in, wid_in, w_in, bias_in, out,
    xp, lsend, rsend, lrecv, rrecv, corner, disc, polar, wid, bias, wall, whi, wlo,
    flip_main, flip_edge, main, edge, band, xz, prow, shift_a, shift_b, chi, clo, mixp, rs,
    lsem, halo_s, halo_r, wsem_s, wsem_r, zsem_s, zsem_r, rsem_s, rsem_r, known, hello, near, seam,
):
    lat, lon = lax.axis_index("lat"), lax.axis_index("lon")
    z, g = lon // PLANE, lon % PLANE
    before, after = (lon + LON - 1) % LON, (lon + 1) % LON
    sibling = lat + 1 - 2 * (lat % 2)
    across = ((lat + 2) % LAT, lon + 1 - 2 * (lon % 2))
    south = lat // (LAT - 1)
    has_up, has_down = lat > 0, lat < LAT - 1
    first, last = lon == 0, lon == LON - 1
    is_polar = (lat == 0) | (lat == LAT - 1)
    up, down = jnp.maximum(lat - 1, 0), jnp.minimum(lat + 1, LAT - 1)

    def local(src, dst, n):
        return pltpu.make_async_copy(src, dst, lsem.at[n])

    source_row = south * (ROWS - 4)
    load_x = local(atm, xp.at[pl.ds(2, ROWS)], 0)
    load_w = local(w_in.at[0], wall.at[:, pl.ds(pl.multiple_of(64 * lat, 64), 64)], 1)
    load_d = local(disc_in, disc, 2)
    load_wid = local(wid_in, wid, 3)
    load_p = local(polar_in.at[south], polar, 4)
    load_b = local(bias_in, bias, 6)
    load_z = local(atm.at[pl.ds(source_row, 4)], xz.at[:, z], 5)

    def remote(src, dst, s, r, device):
        return pltpu.make_async_remote_copy(src, dst, s, r, device_id=device, device_id_type=MESH)

    def ring(d):
        return (lat, ((z + d) % RING) * PLANE + g)

    def plane(d):
        return (lat, z * PLANE + (g + d) % PLANE)

    barrier = pltpu.get_barrier_semaphore()

    def greet(device):
        pl.semaphore_signal(barrier, inc=1, device_id=device, device_id_type=MESH)

    late = z >= RING // 2
    turn = PLANE - 1 - 2 * g
    turning = is_polar & ((g == 0) | (g == PLANE - 1))

    even = lon % 2 == 0
    above, below = lat == LAT - 1, lat != LAT - 2
    neighbours = [
        (jnp.logical_not(last), even, (lat, after)),
        (jnp.logical_not(first), even, (lat, before)),
        (has_up, above, (up, lon)),
        (has_down, below, (down, lon)),
        (has_up & jnp.logical_not(last), above | ((lat == 2) & even), (up, after)),
        (has_down & jnp.logical_not(last), (lat == 0) | (below & even), (down, after)),
        (has_up & jnp.logical_not(first), above | ((lat == 2) & even), (up, before)),
        (has_down & jnp.logical_not(first), (lat == 0) | (below & even), (down, before)),
        (lat >= 0, is_polar, across),
        (turning, g == 0, (lat, lon + turn)),
    ]

    def count(*conditions):
        return sum(c.astype(jnp.int32) for c in conditions)

    @pl.when(is_polar)
    def _():
        load_z.start()

    for there, later, device in neighbours:

        @pl.when(there & later)
        def _(device=device):
            greet(device)

    for there, row in ((first, lat), (first & has_up, up), (first & has_down, down)):

        @pl.when(there)
        def _(row=row):
            greet((row, before))

    @pl.when(is_polar)
    def _():
        for d in range(1, RING):

            @pl.when(z + d < RING)
            def _(d=d):
                greet(ring(d))

    load_x.start()

    def prepare_base():
        load_d.wait()
        load_wid.wait()
        build_base(disc, wid, flip_main, flip_edge, main, edge)

    def prepare_band():
        build_band(main, edge, band)

    def prepare_polar():
        load_p.wait()
        build_shifts(polar, prow, shift_a, shift_b, z)
        build_circular(shift_a, shift_b, chi, clo, g, south)

    greeted = count(*[there & jnp.logical_not(later) for there, later, _ in neighbours])
    greeted += count(last, last & has_up, last & has_down) + z * count(is_polar)

    @pl.when(greeted > 0)
    def _():
        pl.semaphore_wait(barrier, greeted)

    def gather(d):
        return remote(xz.at[:, z], xz.at[:, z], zsem_s.at[d], zsem_r, ring(d))

    def shard(k, n, source_lat, device):
        rows = pl.ds(pl.multiple_of(64 * source_lat, 64), 64)
        source = wall.at[k, rows] if n == 2 else w_in.at[0, k]
        return remote(source, wall.at[k, rows], wsem_s.at[k, n], wsem_r.at[k, n], device)

    own_across = [shard(k, 0, lat, across) for k in range(BASES)]
    own_sibling = [shard(k, 1, lat, (sibling, lon)) for k in range(BASES)]
    passed_on = [shard(k, 2, (lat + 2) % LAT, (sibling, lon)) for k in range(BASES)]
    to_left = remote(lsend, rrecv, halo_s.at[0], halo_r.at[0], (lat, before))
    to_right = remote(rsend, lrecv, halo_s.at[1], halo_r.at[1], (lat, after))
    to_up = [
        remote(atm.at[pl.ds(0, 2)], xp.at[pl.ds(ROWS + 2, 2)], halo_s.at[2], halo_r.at[2], (up, lon)),
        remote(lsend.at[0], corner.at[3], halo_s.at[3], halo_r.at[3], (up, before)),
        remote(rsend.at[0], corner.at[2], halo_s.at[4], halo_r.at[4], (up, after)),
    ]
    to_down = [
        remote(atm.at[pl.ds(ROWS - 2, 2)], xp.at[pl.ds(0, 2)], halo_s.at[5], halo_r.at[5], (down, lon)),
        remote(lsend.at[GROUPS - 1], corner.at[1], halo_s.at[6], halo_r.at[6], (down, before)),
        remote(rsend.at[GROUPS - 1], corner.at[0], halo_s.at[7], halo_r.at[7], (down, after)),
    ]

    @pl.when(is_polar)
    def _():
        load_z.wait()
        for d in range(1, RING):

            @pl.when(z + d >= RING)
            def _(d=d):
                gather(d).start()

        for d in range(1, RING):

            @pl.when(z + d >= RING)
            def _(d=d):
                pl.semaphore_signal(hello.at[d], inc=1, device_id=ring(d), device_id_type=MESH)

    for there, later, device in neighbours:

        @pl.when(there & jnp.logical_not(later))
        def _(device=device):
            pl.semaphore_signal(near, inc=1, device_id=device, device_id_type=MESH)

    @pl.when(last)
    def _():
        pl.semaphore_signal(seam.at[0], inc=1, device_id=(lat, after), device_id_type=MESH)

    @pl.when(last & has_up)
    def _():
        pl.semaphore_signal(seam.at[2], inc=1, device_id=(up, after), device_id_type=MESH)

    @pl.when(last & has_down)
    def _():
        pl.semaphore_signal(seam.at[1], inc=1, device_id=(down, after), device_id_type=MESH)

    for c in (load_w, load_d, load_wid, load_b):
        c.start()

    pl.when(is_polar)(load_p.start)
    load_x.wait()
    pack(xp, lsend, rsend)
    to_come = count(*[there & later for there, later, _ in neighbours])

    @pl.when(to_come > 0)
    def _():
        pl.semaphore_wait(near, to_come)

    for c in own_across:
        c.start()

    held_right = late & (g == PLANE - 1) & jnp.logical_not(last)
    held_left = (late & (g == 0)) | last

    @pl.when(jnp.logical_not(held_right))
    def _():
        to_right.start()

    @pl.when(jnp.logical_not(first | held_left))
    def _():
        to_left.start()

    for c in own_sibling:
        c.start()

    for there, copies in ((has_up, to_up), (has_down, to_down)):

        @pl.when(there)
        def _(copies=copies):
            copies[0].start()
            copies[2].start()

        @pl.when(there & jnp.logical_not(first))
        def _(copies=copies):
            copies[1].start()

    def step_out(n):
        for side in range(2):
            there = plane(2**n if side == 0 else PLANE - 2**n)
            pl.semaphore_signal(known.at[n, side], inc=1, device_id=there, device_id_type=MESH)

    def step_in(n):
        for side in range(2):
            pl.semaphore_wait(known.at[n, side], 1)

    def answer():
        for d in range(RING - 1, 0, -1):

            @pl.when(z < d)
            def _(d=d):
                pl.semaphore_wait(hello.at[d], 1)
                gather(RING - d).start()

    @pl.when(is_polar)
    def _():
        step_out(0)

    prepare_base()

    @pl.when(is_polar)
    def _():
        step_in(0)
        step_out(1)

    prepare_band()

    @pl.when(is_polar)
    def _():
        step_in(1)
        step_out(2)

    @pl.when(is_polar)
    def _():
        pl.when(z >= RING // 2 - 1)(answer)
        prepare_polar()
        pl.when(z < RING // 2 - 1)(answer)

    for c, d in zip(own_across, passed_on):
        c.wait_recv()
        d.start()

    for n, there, copy in ((0, first, to_left), (1, first & has_up, to_up[1]), (2, first & has_down, to_down[1])):

        @pl.when(there)
        def _(n=n, copy=copy):
            pl.semaphore_wait(seam.at[n], 1)
            copy.start()

    pl.when(held_right)(to_right.start)
    pl.when(held_left)(to_left.start)
    load_w.wait()
    for k in range(BASES):
        own_sibling[k].wait_recv()
        passed_on[k].wait_recv()
        hi, lo = split(wall[k])
        whi[CH * k : CH * k + CH, :] = hi
        wlo[CH * k : CH * k + CH, :] = lo

    def mix(taps):
        return dot3(split(taps), (whi[...], wlo[...]))

    def partial(n):
        d = distance(n)
        return remote(mixp.at[pl.ds(16 * n, 16)], rs.at[n], rsem_s, rsem_r, plane(d))

    def partials():
        rows = rs.at[pl.ds(0, PLANE - 1)]
        return remote(rows, rows, rsem_s, rsem_r, plane(1))

    @pl.when(is_polar)
    def _():
        rows = xz.at[:, pl.ds(0, RING - 1)]
        remote(rows, rows, zsem_s.at[0], zsem_r, ring(1)).wait_recv()
        sources = split(xz[...].reshape(CH, CH))
        step_in(2)
        for half in range(2):
            rows = slice(128 * half, 128 * half + 128)
            taps = [dot3((chi[k, rows], clo[k, rows]), sources) for k in range(BASES)]
            mixp[rows] = mix(jnp.concatenate(taps, axis=1))
            for n in range(8 * half, min(8 * half + 8, PLANE - 1)):
                partial(n).start()

    to_right.wait_recv()
    to_left.wait_recv()
    sub = iota((8, CH), 0)

    @pl.when(has_up)
    def _():
        for c in to_down:
            c.wait_recv()
        lrecv[0] = jnp.where(sub < 4, corner[0], lrecv[0])
        rrecv[0] = jnp.where(sub < 4, corner[1], rrecv[0])

    @pl.when(jnp.logical_not(has_up))
    def _():
        xp[0:2] = jnp.zeros((2, COLS, CH), F32)

    @pl.when(has_down)
    def _():
        for c in to_up:
            c.wait_recv()
        lrecv[GROUPS - 1] = jnp.where(sub < 4, lrecv[GROUPS - 1], corner[2])
        rrecv[GROUPS - 1] = jnp.where(sub < 4, rrecv[GROUPS - 1], corner[3])

    @pl.when(jnp.logical_not(has_down))
    def _():
        xp[ROWS + 2 : ROWS + 4] = jnp.zeros((2, COLS, CH), F32)

    load_b.wait()
    shift = bias[...]
    empty = jnp.zeros((16, CH), F32)
    for s in range(TILES):
        x = jnp.concatenate(
            [
                xp[TILE * s : TILE * s + TILE + 4].reshape(160, CH),
                lrecv[4 * s : 4 * s + 5].reshape(40, CH),
                rrecv[4 * s : 4 * s + 5].reshape(40, CH),
                empty,
            ],
            axis=0,
        )
        tile = dot3(split(band[s]), split(x))
        mixed = mix(jnp.concatenate([tile[128 * k : 128 * k + 128] for k in range(BASES)], axis=1))
        out[TILE * s : TILE * s + TILE] = gelu(mixed + shift).reshape(TILE, COLS, CH)

    for c in own_across + own_sibling + passed_on + [to_left, to_right]:
        c.wait_send()

    @pl.when(has_up)
    def _():
        for c in to_up:
            c.wait_send()

    @pl.when(has_down)
    def _():
        for c in to_down:
            c.wait_send()

    @pl.when(is_polar)
    def _():
        for d in range(1, RING):
            gather(d).wait_send()
        partials().wait_send()

    @pl.when(is_polar)
    def _():
        total = mixp[16 * PLANE - 16 : 16 * PLANE, :]
        partials().wait_recv()
        for n in range(PLANE - 1):
            total = total + rs[n]
        total = gelu(total + shift)
        for p in range(2):
            out[p + south * (ROWS - 1 - 2 * p)] = total[8 * p : 8 * p + 8]


def on_device(atmosphere, disc_basis, polar_basis, widths, weights, channel_bias):
    anywhere = pl.BlockSpec(memory_space=pltpu.MemorySpace.HBM)

    def in_hbm(x):
        return pltpu.with_memory_space_constraint(x, pltpu.MemorySpace.HBM)


    def vmem(*shape, dtype=F32):
        return pltpu.VMEM(shape, dtype)

    dma = pltpu.SemaphoreType.DMA
    return pl.pallas_call(
        kernel,
        out_shape=pltpu.VMEM((ROWS, COLS, CH), F32),
        in_specs=[anywhere] * 6,
        out_specs=pl.BlockSpec(memory_space=pltpu.VMEM),
        scratch_shapes=[
            vmem(ROWS + 4, COLS, CH),
            vmem(GROUPS, 8, CH),
            vmem(GROUPS, 8, CH),
            vmem(GROUPS, 8, CH),
            vmem(GROUPS, 8, CH),
            vmem(4, 8, CH),
            vmem(5, 5, BASES, ROWS),
            vmem(BASES, 2, 4, 1024),
            vmem(1, ROWS, dtype=jnp.int32),
            vmem(1, CH),
            vmem(BASES, CH, CH),
            vmem(BASES * CH, CH, dtype=BF16),
            vmem(BASES * CH, CH, dtype=BF16),
            vmem(BASES, 128, 128),
            vmem(BASES, 128, 128),
            vmem(BASES, ROWS, 128),
            vmem(BASES, ROWS, 128),
            vmem(TILES, BASES * TILE * 8, 256),
            vmem(4, RING, 8, CH),
            vmem(24, 1024),
            vmem(2 * PLANE, 24, 128),
            vmem(2 * PLANE, 24, 128),
            vmem(BASES, 256, 256, dtype=BF16),
            vmem(BASES, 256, 256, dtype=BF16),
            vmem(256, CH),
            vmem(PLANE, 16, CH),
            dma((7,)),
            dma((8,)),
            dma((8,)),
            dma((BASES, 3)),
            dma((BASES, 3)),
            dma((RING,)),
            dma,
            dma,
            dma,
            pltpu.SemaphoreType.REGULAR((3, 2)),
            pltpu.SemaphoreType.REGULAR((RING,)),
            pltpu.SemaphoreType.REGULAR,
            pltpu.SemaphoreType.REGULAR((3,)),
        ],
        compiler_params=pltpu.CompilerParams(
            collective_id=0, has_side_effects=True, vmem_limit_bytes=32 * 1024 * 1024
        ),
        name="disco",
    )(
        in_hbm(atmosphere),
        in_hbm(jnp.transpose(disc_basis, (2, 3, 0, 1))),
        in_hbm(polar_basis),
        in_hbm(widths.reshape(1, ROWS)),
        in_hbm(weights),
        in_hbm(channel_bias),
    )


def solution(mesh):
    return jax.shard_map(
        on_device,
        mesh=mesh,
        in_specs=(
            P("lat", "lon", None),
            P(None, "lat", None, None),
            P(),
            P("lat"),
            P(None, None, "lat", None),
            P(),
        ),
        out_specs=P("lat", "lon", None),
        check_vma=False,
    )
```
